128 devices in a mesh: section: 4 (over z_lo, core), dp: 16 (over x, y), tensor: 2 (over z_hi).
Axes of the slice: x: 4, y: 4, z: 4 (z_hi: 2, z_lo: 2; z = z_hi * 2 + z_lo), core: 2. Of those that a mesh axis runs over, the one named last changes fastest.
Arguments:
- layer_inputs: bfloat16 [4, 2, 2048, 8192], P('section', None, 'dp'), may hold values from -6 to 6
- value_cotangent: bfloat16 [4, 2, 2048, 1024], P('section', None, 'dp', 'tensor'), may hold values from -6 to 6
- value_weight: bfloat16 [4, 8192, 1024], P('section', 'dp', 'tensor'), may hold values from -0.0625 to 0.0625
- norm_gain: float32 [4, 8192], P('section'), may hold values from 0.25 to 1.75
- skip_keep: int32 [4, 2, 16], P('section', None, 'dp'), may hold values from 0 to 1, as said below
- top_grad: bfloat16 [2, 2048, 8192], P(None, 'dp', 'tensor'), may hold values from -6 to 6
Outputs:
- section_grads: float32 [4, 2, 2048, 8192], P('section', None, 'dp', 'tensor')
- weight_grad: float32 [4, 8192, 1024], P('section', 'dp', 'tensor')
The draws below stay inside these ranges and needn't reach their ends.
Inputs may be any that keep to these rules, and one draw needn't show every extreme that they name: `skip_keep`: 1 keeps a block of 128 consecutive rows in a layer, 0 lets it bypass the layer.
All inputs are finite; a program needn't handle non-finite values.
Results may differ from the reference program's by a relative error of at most 0.0029.
Values may be sent and summed in bfloat16 or wider, within the bound.
A program may use at most 128 MiB of HBM per device.

```python
import jax
import jax.numpy as jnp
from jax import lax

D = 8192
KV = 1024
BLOCK = 128
BLK_DEV = 1
MB = 2
L_SECTION = 1
TOKENS = 2048
BLOCKS = 16
LAYERS = 4
N_SECTION = 4


def draw_skip_keep(key, part):
    key = jax.random.fold_in(key, 7)
    level_key, coin_key = jax.random.split(key)
    replicas = BLOCKS // BLK_DEV
    levels = jax.random.randint(level_key, (LAYERS, 1, replicas, 1), 1, 4)
    coins = jax.random.randint(coin_key, (LAYERS, MB, replicas, BLK_DEV), 0, 4)
    kept = jnp.where(coins < levels, 1, 0).astype(jnp.int32)
    return kept.reshape(LAYERS, MB, BLOCKS)


def level_of(rng, shape, pieces, least, top_value):
    def one(axis_at, parts):
        draws = jax.random.uniform(jax.random.fold_in(jax.random.fold_in(rng, 6), axis_at), (parts,), jnp.float32, least / len(pieces), top_value / len(pieces))
        return jnp.repeat(jnp.exp(draws), shape[axis_at] // parts).reshape((-1,) + (1,) * (len(shape) - axis_at - 1))

    level = one(*pieces[0])
    for cut in pieces[1:]:
        level = level * one(*cut)
    return level


def normal_values(stream_key, extent, scale, bound, cuts=(), kind=jnp.bfloat16):
    values = scale * jax.random.normal(stream_key, extent, jnp.float32)
    if cuts:
        values = values * level_of(stream_key, extent, cuts, -0.22, 0.18)
    return jnp.clip(values, -bound, bound).astype(kind)


def setup_inputs(seed: int = 0) -> dict:
    key_of = jax.random.split(jax.random.key(seed), 7)
    return {
        "layer_inputs": normal_values(key_of[0], (LAYERS, MB, TOKENS, D), 1.0, 6.0, ((0, 4), (2, 16))),
        "value_cotangent": normal_values(key_of[1], (LAYERS, MB, TOKENS, KV), 1.0, 6.0, ((0, 4), (2, 16), (3, 2))),
        "value_weight": normal_values(key_of[2], (LAYERS, D, KV), D ** -0.5, 0.0625, ((0, 4), (1, 16), (2, 2))),
        "norm_gain": jnp.clip(1.0 + 0.15 * jax.random.normal(key_of[3], (LAYERS, D), jnp.float32), 0.25, 1.75),
        "skip_keep": draw_skip_keep(jax.random.fold_in(key_of[6], 71), 0),
        "top_grad": normal_values(key_of[5], (MB, TOKENS, D), 1.0, 6.0, ((1, 16), (2, 2))),
    }


EPSILON = 1e-05

def branch_back(inputs, cotangent, weight, gain, keep_blocks, running):
    inputs_f = inputs.astype(jnp.float32)
    inverse = lax.rsqrt(lax.optimization_barrier(jnp.mean(inputs_f * inputs_f, axis=-1, keepdims=True)) + EPSILON)
    normed_grad = lax.dot_general(cotangent, weight, (((1,), (1,)), ((), ())), preferred_element_type=jnp.float32)
    scaled = gain * normed_grad
    row_dot = lax.optimization_barrier(jnp.sum(inputs_f * scaled, axis=-1, keepdims=True))
    branch = inverse * scaled - inputs_f * inverse ** 3 * row_dot / D
    row_keep = jnp.repeat(keep_blocks.astype(jnp.float32), BLOCK)[:, None]
    return running + row_keep * branch

def reference(layer_inputs, value_cotangent, value_weight, norm_gain, skip_keep, top_grad):
    running = [top_grad[batch_no].astype(jnp.float32) for batch_no in range(MB)]
    section_out = [None] * N_SECTION
    for section_no in reversed(range(N_SECTION)):
        for layer_no in reversed(range(L_SECTION)):
            index = section_no * L_SECTION + layer_no
            running = [branch_back(layer_inputs[index, batch_no], value_cotangent[index, batch_no], value_weight[index], norm_gain[index], skip_keep[index, batch_no], running[batch_no]) for batch_no in range(MB)]
        section_out[section_no] = jnp.stack(running)
    factor = float(MB * TOKENS) ** (-0.5)
    grads_out = []
    for index in range(LAYERS):
        inputs_f = layer_inputs[index].astype(jnp.float32)
        inverse = lax.rsqrt(lax.optimization_barrier(jnp.mean(inputs_f * inputs_f, axis=-1, keepdims=True)) + EPSILON)
        normed = (inputs_f * inverse * norm_gain[index]).astype(jnp.bfloat16).reshape(MB * TOKENS, D)
        keep_rows = jnp.repeat(skip_keep[index].astype(jnp.float32), BLOCK, axis=1)[..., None]
        masked = (value_cotangent[index].astype(jnp.float32) * keep_rows).astype(jnp.bfloat16).reshape(MB * TOKENS, KV)
        summed = lax.dot_general(normed, masked, (((0,), (0,)), ((), ())), preferred_element_type=jnp.float32)
        grads_out.append(summed * factor)
    return (jnp.stack(section_out), jnp.stack(grads_out))
```

```python
import functools

import jax
import jax.numpy as jnp
from jax import lax
from jax.experimental import pallas as pl
from jax.experimental.pallas import tpu as pltpu
from jax.sharding import PartitionSpec as P

EPSILON = 1e-05
MESH = pl.DeviceIdType.MESH
MB = 2
ROWS = 128
D = 8192
SUB = 1024
HALF = 512
ORDER = (2, 1, 3)
F32 = jnp.float32
BF16 = jnp.bfloat16


def nt(a, b):
    return lax.dot_general(a, b, (((1,), (1,)), ((), ())), preferred_element_type=F32)


def tn(a, b):
    return lax.dot_general(a, b, (((0,), (0,)), ((), ())), preferred_element_type=F32)


def exact(a, b, dims):
    return lax.dot_general(
        a, b, (dims, ((), ())), preferred_element_type=F32, precision=lax.Precision.HIGHEST
    )


def kernel(
    x_hbm, c_hbm, w_hbm, gain, keep,
    s_out, w_out,
    cot, cg, wg, xg, scaled, normed, acc, stat, wp, rsb, rsr, fb, sb, ci,
    loc, zs, zr, cs, cr, xs, xr, ps, pr, ws, wr, ts, tr, hs, hr, as_, ar, rs, rr, bs, br,
):
    sec = lax.axis_index("section")
    dp = lax.axis_index("dp")
    t = lax.axis_index("tensor")
    x, y = dp // 4, dp % 4

    def at(nx, ny, ntensor):
        return (sec, nx * 4 + ny, ntensor)

    def xp(k):
        return at((x + k) % 4, y, t)

    def yp(k):
        return at(x, (y + k) % 4, t)

    zp = at(x, y, 1 - t)
    to = at(2 * (x % 2) + y // 2, 2 * (1 - t) + y % 2, x // 2)
    back = at(2 * t + x // 2, 2 * (x % 2) + y % 2, 1 - y // 2)
    stat_peers = [(k, e) for e in (0, 1) for k in (2, 1, 3, 0) if (k, e) != (0, 0)]

    def remote(src, dst, ssem, rsem, dev):
        return pltpu.make_async_remote_copy(
            src_ref=src, dst_ref=dst, send_sem=ssem, recv_sem=rsem, device_id=dev,
            device_id_type=MESH,
        )

    sub = pl.multiple_of(t * 4096 + x * SUB, SUB)
    own_c = pltpu.make_async_copy(c_hbm.at[0], cot, loc.at[0])
    own_c.start()
    own_x = []
    for m in range(MB):
        cp = pltpu.make_async_copy(
            x_hbm.at[0, m, :, pl.ds(sub, SUB)], xg.at[m, x], loc.at[1 + m]
        )
        cp.start()
        own_x.append(cp)

    barrier = pltpu.get_barrier_semaphore()
    peers = [at((x + k) % 4, y, (t + e) % 2) for k, e in stat_peers]
    peers += [yp(k) for k in ORDER] + [to, back]
    peers += [((sec + 1) % 4, dp, t), ((sec + 3) % 4, dp, t)]
    for dev in peers:
        pl.semaphore_signal(barrier, inc=1, device_id=dev, device_id_type=MESH)
    own_c.wait()
    for m in range(MB):
        kept = keep[0, m, 0].astype(F32)
        cg[m, t, x] = (cot[m].astype(F32) * kept).astype(BF16)
    pl.semaphore_wait(barrier, len(peers))

    sends = []

    def go(cp):
        cp.start()
        sends.append(cp)
        return cp

    wto = remote(w_hbm.at[0], wg.at[2 * (1 - t) + y % 2], ps.at[0], pr.at[0], to)
    go(wto)
    zc = [
        go(remote(cg.at[m, t, x], cg.at[m, t, x], zs.at[m], zr.at[m], zp)) for m in range(MB)
    ]
    cgat = {}
    xat = {}

    def gather_cot(m, half, col):
        for i, k in enumerate(ORDER):
            cgat[m, half, i] = go(
                remote(cg.at[m, col, x], cg.at[m, col, x], cs.at[m, half, i], cr.at[m, half, i], xp(k))
            )

    def send_x(m):
        for i, k in enumerate(ORDER):
            start = pl.multiple_of(t * 4096 + ((x + k) % 4) * SUB, SUB)
            xat[m, i] = go(
                remote(
                    x_hbm.at[0, m, :, pl.ds(start, SUB)], xg.at[m, x], xs.at[m, i], xr.at[m, i], xp(k)
                )
            )

    gather_cot(0, 0, t)
    gather_cot(1, 0, t)
    send_x(0)
    for m in range(MB):
        zc[m].wait_recv()
        gather_cot(m, 1, 1 - t)
    send_x(1)
    wto.wait_recv()
    wgat = [
        go(remote(wg.at[y], wg.at[y], ws.at[i], wr.at[i], yp(k))) for i, k in enumerate(ORDER)
    ]

    lane_row = lax.broadcasted_iota(jnp.int32, (8, 128), 0)
    top_rows = jnp.where(lane_row < 4, 1.0, 0.0).astype(F32)
    low_rows = 1.0 - top_rows
    first_row = jnp.where(lane_row == 0, 1.0, 0.0).astype(F32)
    me = 2 * x + t

    def multiply(m):
        for half in range(2):
            for i in range(3):
                cgat[m, half, i].wait_recv()
        if m == 0:
            for cp in wgat:
                cp.wait_recv()
        own_x[m].wait()
        for i in range(3):
            xat[m, i].wait_recv()
        acc[...] = jnp.zeros_like(acc)

        def tile(i, carry):
            j = i // 2
            rows = pl.ds(pl.multiple_of((i % 2) * 256, 256), 256)
            cols = pl.ds(pl.multiple_of(i * 256, 256), 256)
            ng = nt(cg[m, 0].reshape(HALF, HALF), wg[2 + j, rows, :])
            ng += nt(cg[m, 1].reshape(HALF, HALF), wg[j, rows, :])
            g = gain[0:1, pl.ds(pl.multiple_of(sub + i * 256, 256), 256)]
            sc = ng * g
            scaled[m, :, cols] = sc
            xf = xg[m, :, :, cols].reshape(HALF, 256).astype(F32)
            pr_ = xf * sc
            sq = xf * xf
            acc[0] += pr_[:, :128] + pr_[:, 128:]
            acc[1] += sq[:, :128] + sq[:, 128:]
            return carry

        lax.fori_loop(0, 4, tile, 0)
        stat[m, me] = exact(top_rows, acc[0], ((1,), (1,))) + exact(low_rows, acc[1], ((1,), (1,)))
        return [
            go(
                remote(
                    stat.at[m, me], stat.at[m, me], ts.at[m, i], tr.at[m, i],
                    at((x + k) % 4, y, (t + e) % 2),
                )
            )
            for i, (k, e) in enumerate(stat_peers)
        ]

    def branch(m, arrivals):
        for cp in arrivals:
            cp.wait_recv()
        total = jnp.sum(stat[m], axis=0)
        dot_row = total[0:1]
        inv_row = lax.rsqrt(total[4:5] * (1.0 / D) + EPSILON)
        coef_row = inv_row * inv_row * inv_row * dot_row * (1.0 / D)
        acc[0] = exact(jnp.broadcast_to(inv_row, (8, HALF)), first_row, ((0,), (0,)))
        acc[1] = exact(jnp.broadcast_to(coef_row, (8, HALF)), first_row, ((0,), (0,)))

        def tile(i, carry):
            cols = pl.ds(pl.multiple_of(i * 128, 128), 128)
            g = gain[0:1, pl.ds(pl.multiple_of(sub + i * 128, 128), 128)]
            xf = xg[m, :, :, cols].reshape(HALF, 128).astype(F32)
            scaled[m, :, cols] = acc[0] * scaled[m, :, cols] - xf * acc[1]
            normed[m, :, cols] = (xf * acc[0] * g).astype(BF16)
            return carry

        lax.fori_loop(0, 8, tile, 0)

    below = (sec - 1, dp, t)
    chained = []
    final = {}

    def chain(m):
        for i, k in enumerate((2, 1, 3, 0)):
            xb = (x + k) % 4
            b = m * 4 + i
            cp = remote(sb.at[m, xb], ci.at[b], hs.at[b], hr.at[b], below)
            block = scaled.at[m, pl.ds(pl.multiple_of(xb * ROWS, ROWS), ROWS)]

            @pl.when(sec < 3)
            def _():
                cp.wait_recv()
                sb[m, xb] = (block[...] + ci[b].astype(F32)).astype(BF16)

            @pl.when(sec == 3)
            def _():
                sb[m, xb] = block[...].astype(BF16)

            @pl.when(sec > 0)
            def _():
                cp.start()

            chained.append(cp)
            spot = s_out.at[m, :, pl.ds(pl.multiple_of(x * SUB, SUB), SUB)]
            if k:
                final[m, i] = go(remote(sb.at[m, xb], spot, as_.at[m, i], ar.at[m, i], xp(k)))
            else:
                own = pltpu.make_async_copy(sb.at[m, xb], spot, loc.at[1 + m])
                own.start()
                final[m, i] = own

    def weights():
        def tile(i, carry):
            j = i // 2
            rows = pl.ds(pl.multiple_of((i % 2) * 256, 256), 256)
            cols = pl.ds(pl.multiple_of(i * 256, 256), 256)
            for c in range(2):
                part = tn(normed[0, :, cols], cg[0, c].reshape(HALF, HALF))
                part += tn(normed[1, :, cols], cg[1, c].reshape(HALF, HALF))
                wp[2 * (1 - c) + j, rows, :] = part
                rsb[2 * (1 - c) + j, rows, :] = part.astype(BF16)
            return carry

        lax.fori_loop(0, 4, tile, 0)
        return [
            go(remote(rsb.at[(y + k) % 4], rsr.at[i], rs.at[i], rr.at[i], yp(k)))
            for i, k in enumerate(ORDER)
        ]

    branch(0, multiply(0))
    chain(0)
    branch(1, multiply(1))
    reduced = weights()
    chain(1)
    for cp in reduced:
        cp.wait_recv()
    fb[...] = (
        wp[y] + rsr[0].astype(F32) + rsr[1].astype(F32) + rsr[2].astype(F32)
    ).astype(BF16)
    wback = go(remote(fb, w_out, bs.at[0], br.at[0], back))
    for m in range(MB):
        for i in range(3):
            final[m, i].wait_recv()
        final[m, 3].wait()
    wback.wait_recv()
    for cp in sends:
        cp.wait_send()
    for cp in chained:

        @pl.when(sec > 0)
        def _():
            cp.wait_send()


def on_device(layer_inputs, value_cotangent, value_weight, norm_gain, skip_keep, top_grad):
    any_ = pl.BlockSpec(memory_space=pl.ANY)
    dma = pltpu.SemaphoreType.DMA
    sums, weight = pl.pallas_call(
        kernel,
        name="backward",
        out_shape=(
            jax.ShapeDtypeStruct((MB, ROWS, 4096), BF16),
            jax.ShapeDtypeStruct((HALF, HALF), BF16),
        ),
        in_specs=[
            any_, any_, any_,
            pl.BlockSpec(memory_space=pltpu.VMEM),
            pl.BlockSpec(memory_space=pltpu.SMEM),
        ],
        out_specs=(any_, any_),
        scratch_shapes=[
            pltpu.VMEM((MB, ROWS, HALF), BF16),
            pltpu.VMEM((MB, 2, 4, ROWS, HALF), BF16),
            pltpu.VMEM((4, HALF, HALF), BF16),
            pltpu.VMEM((MB, 4, ROWS, SUB), BF16),
            pltpu.VMEM((MB, HALF, SUB), F32),
            pltpu.VMEM((MB, HALF, SUB), BF16),
            pltpu.VMEM((2, HALF, 128), F32),
            pltpu.VMEM((MB, 8, 8, HALF), F32),
            pltpu.VMEM((4, HALF, HALF), F32),
            pltpu.VMEM((4, HALF, HALF), BF16),
            pltpu.VMEM((3, HALF, HALF), BF16),
            pltpu.VMEM((HALF, HALF), BF16),
            pltpu.VMEM((MB, 4, ROWS, SUB), BF16),
            pltpu.VMEM((8, ROWS, SUB), BF16),
            dma((3,)),
            dma((MB,)), dma((MB,)),
            dma((MB, 2, 3)), dma((MB, 2, 3)),
            dma((MB, 3)), dma((MB, 3)),
            dma((1,)), dma((1,)),
            dma((3,)), dma((3,)),
            dma((MB, 7)), dma((MB, 7)),
            dma((8,)), dma((8,)),
            dma((MB, 3)), dma((MB, 3)),
            dma((3,)), dma((3,)),
            dma((1,)), dma((1,)),
        ],
        compiler_params=pltpu.CompilerParams(
            collective_id=0, has_side_effects=True, vmem_limit_bytes=56 * 1024 * 1024
        ),
    )(layer_inputs, value_cotangent, value_weight, norm_gain, skip_keep)
    total_rows = MB * ROWS * lax.axis_size("dp")
    factor = float(total_rows) ** (-0.5)
    grads = top_grad.astype(F32) + sums.astype(F32)
    return grads[None], (weight.astype(F32) * factor)[None]


def solution(mesh):
    placed = (
        P("section", None, "dp", None),
        P("section", None, "dp", "tensor"),
        P("section", "dp", "tensor"),
        P("section", None),
        P("section", None, "dp"),
        P(None, "dp", "tensor"),
    )
    return jax.shard_map(
        on_device,
        mesh=mesh,
        in_specs=placed,
        out_specs=(P("section", None, "dp", "tensor"), P("section", "dp", "tensor")),
        check_vma=False,
    )
```

```python
import functools

import jax
import jax.numpy as jnp
from jax import lax
from jax.experimental import pallas as pl
from jax.experimental.pallas import tpu as pltpu
from jax.sharding import PartitionSpec as P

EPSILON = 1e-05
MESH = pl.DeviceIdType.MESH
MB = 2
ROWS = 128
D = 8192
SUB = 1024
HALF = 512
ORDER = (2, 1, 3)
F32 = jnp.float32
BF16 = jnp.bfloat16


def nt(a, b):
    return lax.dot_general(a, b, (((1,), (1,)), ((), ())), preferred_element_type=F32)


def tn(a, b):
    return lax.dot_general(a, b, (((0,), (0,)), ((), ())), preferred_element_type=F32)


def exact(a, b, dims):
    return lax.dot_general(
        a, b, (dims, ((), ())), preferred_element_type=F32, precision=lax.Precision.HIGHEST
    )


def kernel(
    x_hbm, c_hbm, w_hbm, gain, keep,
    s_out, w_out,
    cot, cg, wg, xg, scaled, normed, acc, stat, wp, rsb, opp, rsr, fb, sb, ci,
    loc, zs, zr, cs, cr, xs, xr, ps, pr, ws, wr, ts, tr, hs, hr, as_, ar, os_, or_, rs, rr, bs, br,
):
    sec = lax.axis_index("section")
    dp = lax.axis_index("dp")
    t = lax.axis_index("tensor")
    x, y = dp // 4, dp % 4

    def at(nx, ny, ntensor):
        return (sec, nx * 4 + ny, ntensor)

    def xp(k):
        return at((x + k) % 4, y, t)

    def yp(k):
        return at(x, (y + k) % 4, t)

    def quarter(nx):
        high = (nx // 2 + t) % 2
        return (nx + high) % 2, high

    zp = at(x, y, 1 - t)
    to_t, row_high = x // 2, y // 2
    crosses = (to_t + t) % 2
    to_x = (x + 4 + row_high * (2 * (x % 2) - 1)) % 4
    to_y = y + crosses * (3 - 2 * y)
    to = at(to_x, to_y, to_t)
    chip, high = quarter(x)
    foreign = (y // 2 + high) % 2
    back = at(2 * t + chip, y + foreign * (3 - 2 * y), t + foreign * (1 - 2 * t))
    stays = (crosses + row_high) == 0
    quart = 2 * chip + high
    sub = pl.multiple_of(t * 4096 + quart * SUB, SUB)
    stat_peers = [(k, e) for e in (0, 1) for k in (2, 1, 3, 0) if (k, e) != (0, 0)]

    def shard(slot):
        far = (slot // 2 + high) % 2
        col = t + far * (1 - 2 * t)
        j = (slot + far) % 2
        return col, j

    def slot_of(far, j):
        near = 2 * high + j
        return near + far * (3 - 2 * near)

    def remote(src, dst, ssem, rsem, dev):
        return pltpu.make_async_remote_copy(
            src_ref=src, dst_ref=dst, send_sem=ssem, recv_sem=rsem, device_id=dev,
            device_id_type=MESH,
        )

    own_c = pltpu.make_async_copy(c_hbm.at[0], cot, loc.at[0])
    own_c.start()
    own_x = []
    for m in range(MB):
        cp = pltpu.make_async_copy(
            x_hbm.at[0, m, :, pl.ds(sub, SUB)], xg.at[m, x], loc.at[1 + m]
        )
        cp.start()
        own_x.append(cp)

    barrier = pltpu.get_barrier_semaphore()
    peers = [at((x + k) % 4, y, (t + e) % 2) for k, e in stat_peers]
    peers += [yp(k) for k in ORDER]
    peers += [((sec + 1) % 4, dp, t), ((sec + 3) % 4, dp, t)]
    for dev in peers:
        pl.semaphore_signal(barrier, inc=1, device_id=dev, device_id_type=MESH)

    @pl.when(jnp.logical_not(stays))
    def _():
        for dev in (to, back):
            pl.semaphore_signal(barrier, inc=1, device_id=dev, device_id_type=MESH)

    own_c.wait()
    for m in range(MB):
        kept = keep[0, m].astype(F32)
        cg[m, t, x] = (cot[m].astype(F32) * kept).astype(BF16)
    pl.semaphore_wait(barrier, len(peers) + 2 - 2 * stays.astype(jnp.int32))

    sends = []

    def go(cp):
        cp.start()
        sends.append(cp)
        return cp

    def moved(src, dst, lsem, ssem, rsem, dev):
        local = pltpu.make_async_copy(src, dst, lsem)
        far = remote(src, dst, ssem, rsem, dev)

        @pl.when(stays)
        def _():
            local.start()

        @pl.when(jnp.logical_not(stays))
        def _():
            far.start()

        def arrive():
            @pl.when(stays)
            def _():
                local.wait()

            @pl.when(jnp.logical_not(stays))
            def _():
                far.wait_recv()

        def leave():
            @pl.when(jnp.logical_not(stays))
            def _():
                far.wait_send()

        return arrive, leave

    part = [pl.ds(0, 256), pl.ds(256, 256)]
    left = (x + 3) % 4
    right = (x + 1) % 4
    wmove = [
        moved(w_hbm.at[0, part[h]], wg.at[to_y, part[h]], loc.at[3 + h], ps.at[h], pr.at[h], to)
        for h in range(2)
    ]
    zc = [
        go(remote(cg.at[m, t, x], cg.at[m, t, x], zs.at[m], zr.at[m], zp)) for m in range(MB)
    ]

    def send_cot(m, half, i, col, origin, k):
        return go(
            remote(
                cg.at[m, col, origin], cg.at[m, col, origin],
                cs.at[m, half, i], cr.at[m, half, i], xp(k),
            )
        )

    xat = {}

    def send_x(m):
        for i, k in enumerate(ORDER):
            to_chip, to_high = quarter((x + k) % 4)
            start = pl.multiple_of(t * 4096 + (2 * to_chip + to_high) * SUB, SUB)
            xat[m, i] = go(
                remote(
                    x_hbm.at[0, m, :, pl.ds(start, SUB)], xg.at[m, x], xs.at[m, i], xr.at[m, i], xp(k)
                )
            )

    cat = {}
    for m in range(MB):
        cat[m, 0, 0] = send_cot(m, 0, 0, t, x, 1)
        cat[m, 0, 1] = send_cot(m, 0, 1, t, x, 3)
    got = set()

    def wait_cot(key):
        if key not in got:
            got.add(key)
            cat[key].wait_recv()

    for m in range(MB):
        zc[m].wait_recv()
        cat[m, 1, 0] = send_cot(m, 1, 0, 1 - t, x, 1)
        cat[m, 1, 1] = send_cot(m, 1, 1, 1 - t, x, 3)
    send_x(0)
    for m in range(MB):
        wait_cot((m, 0, 0))
        cat[m, 0, 2] = send_cot(m, 0, 2, t, left, 1)
    wat = {}
    for h in range(2):
        wmove[h][0]()
        for i, k in enumerate((1, 3)):
            wat[h, i] = go(
                remote(wg.at[y, part[h]], wg.at[y, part[h]], ws.at[h, i], wr.at[h, i], yp(k))
            )
    for m in range(MB):
        wait_cot((m, 1, 1))
        cat[m, 1, 2] = send_cot(m, 1, 2, 1 - t, right, 3)
    send_x(1)
    for h, origin, k in ((0, (y + 3) % 4, 1), (1, (y + 1) % 4, 3)):
        wat[h, h].wait_recv()
        wat[h, 2] = go(
            remote(wg.at[origin, part[h]], wg.at[origin, part[h]], ws.at[h, 2], wr.at[h, 2], yp(k))
        )

    lane_row = lax.broadcasted_iota(jnp.int32, (8, 128), 0)
    top_rows = jnp.where(lane_row < 4, 1.0, 0.0).astype(F32)
    low_rows = 1.0 - top_rows
    first_row = jnp.where(lane_row == 0, 1.0, 0.0).astype(F32)
    me = 2 * x + t

    def multiply(m):
        for half in range(2):
            for i in range(3):
                wait_cot((m, half, i))
        if m == 0:
            for key in ((0, 1), (0, 2), (1, 0), (1, 2)):
                wat[key].wait_recv()
        own_x[m].wait()
        for i in range(3):
            xat[m, i].wait_recv()
        acc[...] = jnp.zeros_like(acc)

        def tile(i, carry):
            j = i // 2
            rows = pl.ds(pl.multiple_of((i % 2) * 256, 256), 256)
            cols = pl.ds(pl.multiple_of(i * 256, 256), 256)
            ng = nt(cg[m, t].reshape(HALF, HALF), wg[slot_of(0, j), rows, :])
            ng += nt(cg[m, 1 - t].reshape(HALF, HALF), wg[slot_of(1, j), rows, :])
            g = gain[0:1, pl.ds(pl.multiple_of(sub + i * 256, 256), 256)]
            sc = ng * g
            scaled[m, :, cols] = sc
            xf = xg[m, :, :, cols].reshape(HALF, 256).astype(F32)
            dot = xf * sc
            sq = xf * xf
            acc[0] += dot[:, :128] + dot[:, 128:]
            acc[1] += sq[:, :128] + sq[:, 128:]
            return carry

        lax.fori_loop(0, 4, tile, 0)
        stat[m, me] = exact(top_rows, acc[0], ((1,), (1,))) + exact(low_rows, acc[1], ((1,), (1,)))
        return [
            go(
                remote(
                    stat.at[m, me], stat.at[m, me], ts.at[m, i], tr.at[m, i],
                    at((x + k) % 4, y, (t + e) % 2),
                )
            )
            for i, (k, e) in enumerate(stat_peers)
        ]

    def branch(m, arrivals):
        for cp in arrivals:
            cp.wait_recv()
        total = jnp.sum(stat[m], axis=0)
        dot_row = total[0:1]
        inv_row = lax.rsqrt(total[4:5] * (1.0 / D) + EPSILON)
        coef_row = inv_row * inv_row * inv_row * dot_row * (1.0 / D)
        acc[0] = exact(jnp.broadcast_to(inv_row, (8, HALF)), first_row, ((0,), (0,)))
        acc[1] = exact(jnp.broadcast_to(coef_row, (8, HALF)), first_row, ((0,), (0,)))

        def tile(i, carry):
            cols = pl.ds(pl.multiple_of(i * 128, 128), 128)
            g = gain[0:1, pl.ds(pl.multiple_of(sub + i * 128, 128), 128)]
            xf = xg[m, :, :, cols].reshape(HALF, 128).astype(F32)
            scaled[m, :, cols] = acc[0] * scaled[m, :, cols] - xf * acc[1]
            normed[m, :, cols] = (xf * acc[0] * g).astype(BF16)
            return carry

        lax.fori_loop(0, 8, tile, 0)

    below = (sec - 1, dp, t)
    chained = {}
    final = {}
    spots = (2, 1, 3, 0)
    for m in range(MB):
        for i, k in enumerate(spots):
            xb = (x + k) % 4
            b = m * 4 + i
            chained[m, i] = remote(sb.at[m, xb], ci.at[b], hs.at[b], hr.at[b], below)
            spot = s_out.at[m, :, pl.ds(pl.multiple_of(quart * SUB, SUB), SUB)]
            if k:
                final[m, i] = remote(sb.at[m, xb], spot, as_.at[m, i], ar.at[m, i], xp(k))
            else:
                final[m, i] = pltpu.make_async_copy(sb.at[m, xb], spot, loc.at[1 + m])

    def chain(m):
        for i, k in enumerate(spots):
            xb = (x + k) % 4
            cp = chained[m, i]
            block = scaled.at[m, pl.ds(pl.multiple_of(xb * ROWS, ROWS), ROWS)]

            @pl.when(sec < 3)
            def _():
                cp.wait_recv()
                sb[m, xb] = (block[...] + ci[m * 4 + i].astype(F32)).astype(BF16)

            @pl.when(sec == 3)
            def _():
                sb[m, xb] = block[...].astype(BF16)

            @pl.when(sec > 0)
            def _():
                cp.start()

            final[m, i].start()

    red = {}

    def product(slot, h):
        col, j = shard(slot)
        cols = pl.ds(pl.multiple_of(j * HALF + h * 256, 256), 256)
        total = tn(normed[0, :, cols], cg[0, col].reshape(HALF, HALF))
        total += tn(normed[1, :, cols], cg[1, col].reshape(HALF, HALF))
        return total

    def pass_on(src, dst, i, k):
        return go(remote(src, dst, rs.at[i], rr.at[i], yp(k)))

    down, up, far_y = (y + 3) % 4, (y + 1) % 4, (y + 2) % 4

    def weights():
        for h, k in ((0, 1), (1, 3)):
            rsb[2, h] = product(far_y, h).astype(BF16)
            red["opp", h] = go(remote(rsb.at[2, h], opp.at[h], os_.at[h], or_.at[h], yp(k)))
        for h in (1, 0):
            wp[0, h] = product(up, h)
            wp[1, h] = product(down, h)
            if h == 1:
                rsb[0, 1] = wp[0, 1].astype(BF16)
                red[0, 1] = pass_on(rsb.at[0, 1], rsr.at[0, 1], 1, 1)
            else:
                rsb[1, 0] = wp[1, 0].astype(BF16)
                red[1, 0] = pass_on(rsb.at[1, 0], rsr.at[1, 0], 2, 3)
        for h in range(2):
            wp[2, h] = product(y, h)
        red["opp", 0].wait_recv()
        rsb[0, 0] = (wp[0, 0] + opp[0].astype(F32)).astype(BF16)
        red[0, 0] = pass_on(rsb.at[0, 0], rsr.at[0, 0], 0, 1)
        red["opp", 1].wait_recv()
        rsb[1, 1] = (wp[1, 1] + opp[1].astype(F32)).astype(BF16)
        red[1, 1] = pass_on(rsb.at[1, 1], rsr.at[1, 1], 3, 3)

    def finish():
        moves = []
        for h in range(2):
            red[0, h].wait_recv()
            red[1, h].wait_recv()
            fb[h] = (wp[2, h] + rsr[0, h].astype(F32) + rsr[1, h].astype(F32)).astype(BF16)
            moves.append(
                moved(fb.at[h], w_out.at[part[h]], loc.at[3 + h], bs.at[h], br.at[h], back)
            )
        return moves

    branch(0, multiply(0))

    @pl.when(sec >= 2)
    def _():
        chain(0)

    branch(1, multiply(1))
    weights()

    @pl.when(sec < 2)
    def _():
        chain(0)

    chain(1)
    returned = finish()
    for m in range(MB):
        for i in range(3):
            final[m, i].wait_recv()
            final[m, i].wait_send()
        final[m, 3].wait()
    for arrive, leave in returned:
        arrive()
        leave()
    for _, leave in wmove:
        leave()
    for cp in sends:
        cp.wait_send()
    for cp in chained.values():

        @pl.when(sec > 0)
        def _():
            cp.wait_send()


def on_device(layer_inputs, value_cotangent, value_weight, norm_gain, skip_keep, top_grad):
    any_ = pl.BlockSpec(memory_space=pl.ANY)
    dma = pltpu.SemaphoreType.DMA
    sums, weight = pl.pallas_call(
        kernel,
        name="backward",
        out_shape=(
            jax.ShapeDtypeStruct((MB, ROWS, 4096), BF16),
            jax.ShapeDtypeStruct((HALF, HALF), BF16),
        ),
        in_specs=[
            any_, any_, any_,
            pl.BlockSpec(memory_space=pltpu.VMEM),
            pl.BlockSpec(memory_space=pltpu.SMEM),
        ],
        out_specs=(any_, any_),
        scratch_shapes=[
            pltpu.VMEM((MB, ROWS, HALF), BF16),
            pltpu.VMEM((MB, 2, 4, ROWS, HALF), BF16),
            pltpu.VMEM((4, HALF, HALF), BF16),
            pltpu.VMEM((MB, 4, ROWS, SUB), BF16),
            pltpu.VMEM((MB, HALF, SUB), F32),
            pltpu.VMEM((MB, HALF, SUB), BF16),
            pltpu.VMEM((2, HALF, 128), F32),
            pltpu.VMEM((MB, 8, 8, HALF), F32),
            pltpu.VMEM((3, 2, 256, HALF), F32),
            pltpu.VMEM((3, 2, 256, HALF), BF16),
            pltpu.VMEM((2, 256, HALF), BF16),
            pltpu.VMEM((2, 2, 256, HALF), BF16),
            pltpu.VMEM((2, 256, HALF), BF16),
            pltpu.VMEM((MB, 4, ROWS, SUB), BF16),
            pltpu.VMEM((8, ROWS, SUB), BF16),
            dma((5,)),
            dma((MB,)), dma((MB,)),
            dma((MB, 2, 3)), dma((MB, 2, 3)),
            dma((MB, 3)), dma((MB, 3)),
            dma((2,)), dma((2,)),
            dma((2, 3)), dma((2, 3)),
            dma((MB, 7)), dma((MB, 7)),
            dma((8,)), dma((8,)),
            dma((MB, 3)), dma((MB, 3)),
            dma((2,)), dma((2,)),
            dma((4,)), dma((4,)),
            dma((2,)), dma((2,)),
        ],
        compiler_params=pltpu.CompilerParams(
            collective_id=0, has_side_effects=True, vmem_limit_bytes=56 * 1024 * 1024
        ),
    )(layer_inputs, value_cotangent, value_weight, norm_gain, skip_keep.reshape(1, MB))
    total_rows = MB * ROWS * lax.axis_size("dp")
    factor = float(total_rows) ** (-0.5)
    grads = top_grad.astype(F32) + sums.astype(F32)
    return grads[None], (weight.astype(F32) * factor)[None]


def solution(mesh):
    placed = (
        P("section", None, "dp", None),
        P("section", None, "dp", "tensor"),
        P("section", "dp", "tensor"),
        P("section", None),
        P("section", None, "dp"),
        P(None, "dp", "tensor"),
    )
    return jax.shard_map(
        on_device,
        mesh=mesh,
        in_specs=placed,
        out_specs=(P("section", None, "dp", "tensor"), P("section", "dp", "tensor")),
        check_vma=False,
    )
```

```python
import functools

import jax
import jax.numpy as jnp
from jax import lax
from jax.experimental import pallas as pl
from jax.experimental.pallas import tpu as pltpu
from jax.sharding import PartitionSpec as P

EPSILON = 1e-05
MESH = pl.DeviceIdType.MESH
MB = 2
ROWS = 128
D = 8192
SUB = 1024
HALF = 512
ORDER = (2, 1, 3)
F32 = jnp.float32
BF16 = jnp.bfloat16


def nt(a, b):
    return lax.dot_general(a, b, (((1,), (1,)), ((), ())), preferred_element_type=F32)


def tn(a, b):
    return lax.dot_general(a, b, (((0,), (0,)), ((), ())), preferred_element_type=F32)


def exact(a, b, dims):
    return lax.dot_general(
        a, b, (dims, ((), ())), preferred_element_type=F32, precision=lax.Precision.HIGHEST
    )


def kernel(
    x_hbm, c_hbm, w_hbm, gain, keep,
    s_out, w_out,
    cot, cg, wg, xg, scaled, normed, acc, stat, wp, rsi, opp, rso, rsr, fb, sb, ci,
    loc, zs, zr, cs, cr, xs, xr, ps, pr, ws, wr, ts, tr, hs, hr, as_, ar, os_, or_, rs, rr, bs, br,
):
    sec = lax.axis_index("section")
    dp = lax.axis_index("dp")
    t = lax.axis_index("tensor")
    x, y = dp // 4, dp % 4

    def at(nx, ny, ntensor):
        return (sec, nx * 4 + ny, ntensor)

    def yp(k):
        return at(x, (y + k) % 4, t)

    zp = at(x, y, 1 - t)
    odd = x % 2
    holds = (x // 2) == t
    lacks = jnp.logical_not(holds)
    here = holds.astype(jnp.int32) * (2 * odd - 1) + 1 - odd
    inner = at(x + 1 - 2 * odd, y, t)
    outer = at((x + 3 + 2 * odd) % 4, y, t)
    stat_peers = [(k, e) for e in (0, 1) for k in (2, 1, 3, 0) if (k, e) != (0, 0)]
    part = [pl.ds(0, 256), pl.ds(256, 256)]

    def feature(block, ny):
        return pl.multiple_of(t * 4096 + block * 2048 + ny * HALF, HALF)

    def remote(src, dst, ssem, rsem, dev):
        return pltpu.make_async_remote_copy(
            src_ref=src, dst_ref=dst, send_sem=ssem, recv_sem=rsem, device_id=dev,
            device_id_type=MESH,
        )

    own_c = pltpu.make_async_copy(c_hbm.at[0], cot, loc.at[0])
    own_c.start()
    own_w = pltpu.make_async_copy(w_hbm.at[0], wg.at[here, t], loc.at[1])

    @pl.when(holds)
    def _():
        own_w.start()

    own_x = {}
    for m in range(MB):
        for e in range(2):
            own_x[m, e] = pltpu.make_async_copy(
                x_hbm.at[0, m, :, pl.ds(feature(e, y), HALF)],
                xg.at[m, y, :, pl.ds(e * HALF, HALF)],
                loc.at[2 + 2 * m + e],
            )
            own_x[m, e].start()

    barrier = pltpu.get_barrier_semaphore()
    peers = [at(x, (y + k) % 4, (t + e) % 2) for k, e in stat_peers]
    peers += [inner, outer, ((sec + 1) % 4, dp, t), ((sec + 3) % 4, dp, t)]
    for dev in peers:
        pl.semaphore_signal(barrier, inc=1, device_id=dev, device_id_type=MESH)
    own_c.wait()
    for m in range(MB):
        kept = keep[0, m].astype(F32)
        cg[m, t, y] = (cot[m].astype(F32) * kept).astype(BF16)
    pl.semaphore_wait(barrier, len(peers))

    sends = []

    def go(cp):
        cp.start()
        sends.append(cp)
        return cp

    def send_cot(m, half, i, col, origin, k):
        return go(
            remote(
                cg.at[m, col, origin], cg.at[m, col, origin],
                cs.at[m, half, i], cr.at[m, half, i], yp(k),
            )
        )

    zc = []
    cat = {}
    for m in range(MB):
        zc.append(go(remote(cg.at[m, t, y], cg.at[m, t, y], zs.at[m], zr.at[m], zp)))
        cat[m, 0, 0] = send_cot(m, 0, 0, t, y, 1)
        cat[m, 0, 1] = send_cot(m, 0, 1, t, y, 3)
    got = set()

    def wait_cot(key):
        if key not in got:
            got.add(key)
            cat[key].wait_recv()

    wcross = [
        remote(w_hbm.at[0, part[h]], wg.at[odd, t, part[h]], ps.at[h], pr.at[h], zp)
        for h in range(2)
    ]

    @pl.when(lacks)
    def _():
        for h in range(2):
            wcross[h].start()

    win, wout = {}, {}
    for p in range(2):
        col = t if p == 0 else 1 - t
        for h in range(2):
            block = wg.at[here, col, part[h]]
            win[p, h] = remote(block, block, ws.at[p, h, 0], wr.at[p, h, 0], inner)
            wout[p, h] = remote(block, block, ws.at[p, h, 1], wr.at[p, h, 1], outer)

    def weight_step(p, h):
        @pl.when(holds)
        def _():
            if p == 1:
                wcross[h].wait_recv()
                wout[p, h].start()

        @pl.when(lacks)
        def _():
            wout[p, h].wait_recv()

        go(win[p, h])

    xat = {}

    def send_x(m):
        for i, k in enumerate(ORDER):
            for e in range(2):
                xat[m, i, e] = go(
                    remote(
                        x_hbm.at[0, m, :, pl.ds(feature(e, (y + k) % 4), HALF)],
                        xg.at[m, y, :, pl.ds(e * HALF, HALF)],
                        xs.at[m, i, e], xr.at[m, i, e], yp(k),
                    )
                )

    @pl.when(holds)
    def _():
        own_w.wait()
        wout[0, 0].start()
        wout[0, 1].start()

    up, down = (y + 1) % 4, (y + 3) % 4
    zc[0].wait_recv()
    cat[0, 1, 0] = send_cot(0, 1, 0, 1 - t, y, 1)
    cat[0, 1, 1] = send_cot(0, 1, 1, 1 - t, y, 3)
    wait_cot((0, 0, 0))
    cat[0, 0, 2] = send_cot(0, 0, 2, t, down, 1)
    weight_step(0, 0)
    zc[1].wait_recv()
    cat[1, 1, 0] = send_cot(1, 1, 0, 1 - t, y, 1)
    cat[1, 1, 1] = send_cot(1, 1, 1, 1 - t, y, 3)
    send_x(0)
    wait_cot((1, 0, 0))
    cat[1, 0, 2] = send_cot(1, 0, 2, t, down, 1)
    weight_step(0, 1)
    for m in range(MB):
        wait_cot((m, 1, 1))
        cat[m, 1, 2] = send_cot(m, 1, 2, 1 - t, up, 3)
    send_x(1)
    weight_step(1, 0)
    weight_step(1, 1)

    lane_row = lax.broadcasted_iota(jnp.int32, (8, 128), 0)
    top_rows = jnp.where(lane_row < 4, 1.0, 0.0).astype(F32)
    low_rows = 1.0 - top_rows
    first_row = jnp.where(lane_row == 0, 1.0, 0.0).astype(F32)
    me = 2 * y + t

    def multiply(m):
        for half in range(2):
            for i in range(3):
                wait_cot((m, half, i))
        if m == 0:
            for cp in win.values():
                cp.wait_recv()
        for e in range(2):
            own_x[m, e].wait()
            for i in range(3):
                xat[m, i, e].wait_recv()
        acc[...] = jnp.zeros_like(acc)

        def tile(i, carry):
            rows = pl.ds(pl.multiple_of((i % 2) * 256, 256), 256)
            cols = pl.ds(pl.multiple_of(i * 256, 256), 256)
            ng = nt(cg[m, 0].reshape(HALF, HALF), wg[i // 2, 0, rows, :])
            ng += nt(cg[m, 1].reshape(HALF, HALF), wg[i // 2, 1, rows, :])
            start = pl.multiple_of(feature(i // 2, y) + (i % 2) * 256, 256)
            sc = ng * gain[0:1, pl.ds(start, 256)]
            scaled[m, :, cols] = sc
            xf = xg[m, :, :, cols].reshape(HALF, 256).astype(F32)
            dot = xf * sc
            sq = xf * xf
            acc[0] += dot[:, :128] + dot[:, 128:]
            acc[1] += sq[:, :128] + sq[:, 128:]
            return carry

        lax.fori_loop(0, 4, tile, 0)
        stat[m, me] = exact(top_rows, acc[0], ((1,), (1,))) + exact(low_rows, acc[1], ((1,), (1,)))
        return [
            go(
                remote(
                    stat.at[m, me], stat.at[m, me], ts.at[m, i], tr.at[m, i],
                    at(x, (y + k) % 4, (t + e) % 2),
                )
            )
            for i, (k, e) in enumerate(stat_peers)
        ]

    def branch(m, arrivals):
        for cp in arrivals:
            cp.wait_recv()
        total = jnp.sum(stat[m], axis=0)
        dot_row = total[0:1]
        inv_row = lax.rsqrt(total[4:5] * (1.0 / D) + EPSILON)
        coef_row = inv_row * inv_row * inv_row * dot_row * (1.0 / D)
        acc[0] = exact(jnp.broadcast_to(inv_row, (8, HALF)), first_row, ((0,), (0,)))
        acc[1] = exact(jnp.broadcast_to(coef_row, (8, HALF)), first_row, ((0,), (0,)))

        def tile(i, carry):
            cols = pl.ds(pl.multiple_of(i * 128, 128), 128)
            start = pl.multiple_of(feature(i // 4, y) + (i % 4) * 128, 128)
            g = gain[0:1, pl.ds(start, 128)]
            xf = xg[m, :, :, cols].reshape(HALF, 128).astype(F32)
            scaled[m, :, cols] = acc[0] * scaled[m, :, cols] - xf * acc[1]
            normed[m, :, cols] = (xf * acc[0] * g).astype(BF16)
            return carry

        lax.fori_loop(0, 8, tile, 0)

    below = (sec - 1, dp, t)
    chained = {}
    final = {}
    spots = (2, 1, 3, 0)
    for m in range(MB):
        for i, k in enumerate(spots):
            yb = (y + k) % 4
            b = m * 4 + i
            chained[m, i] = remote(sb.at[m, yb], ci.at[b], hs.at[b], hr.at[b], below)
            for e in range(2):
                src = sb.at[m, yb, :, pl.ds(e * HALF, HALF)]
                spot = s_out.at[m, :, pl.ds(pl.multiple_of(e * 2048 + y * HALF, HALF), HALF)]
                if k:
                    final[m, i, e] = remote(src, spot, as_.at[m, i, e], ar.at[m, i, e], yp(k))
                else:
                    final[m, i, e] = pltpu.make_async_copy(src, spot, loc.at[2 + 2 * m + e])

    def chain(m, i):
        yb = (y + spots[i]) % 4
        cp = chained[m, i]
        block = scaled.at[m, pl.ds(pl.multiple_of(yb * ROWS, ROWS), ROWS)]

        @pl.when(sec < 3)
        def _():
            cp.wait_recv()
            sb[m, yb] = (block[...] + ci[m * 4 + i].astype(F32)).astype(BF16)

        @pl.when(sec == 3)
        def _():
            sb[m, yb] = block[...].astype(BF16)

        @pl.when(sec > 0)
        def _():
            cp.start()

    def deliver(m, i):
        for e in range(2):
            final[m, i, e].start()

    def product(block, p, h):
        col = 1 - t if p == 0 else t
        cols = pl.ds(pl.multiple_of(block * HALF + h * 256, 256), 256)
        total = tn(normed[0, :, cols], cg[0, col].reshape(HALF, HALF))
        total += tn(normed[1, :, cols], cg[1, col].reshape(HALF, HALF))
        return total

    steps = [(p, h) for p in range(2) for h in range(2)]
    rin, rout, ret, kept_here = {}, {}, {}, {}
    for p, h in steps:
        i = 2 * p + h
        rin[p, h] = remote(rsi.at[i], opp.at[i], rs.at[i], rr.at[i], inner)
        rout[p, h] = remote(rso.at[i], rsr.at[i], os_.at[i], or_.at[i], outer)
    for h in range(2):
        ret[h] = remote(fb.at[h], w_out.at[part[h]], bs.at[h], br.at[h], zp)
        kept_here[h] = pltpu.make_async_copy(fb.at[2 + h], w_out.at[part[h]], loc.at[6 + h])

    def weights():
        for p, h in steps:
            i = 2 * p + h
            rsi[i] = product(1 - here, p, h).astype(BF16)
            go(rin[p, h])
            wp[i] = product(here, p, h)

    def relay(p, h):
        i = 2 * p + h
        rin[p, h].wait_recv()

        @pl.when(lacks)
        def _():
            rso[i] = (wp[i] + opp[i].astype(F32)).astype(BF16)
            rout[p, h].start()

    def settle(p, h):
        i = 2 * p + h

        @pl.when(holds)
        def _():
            rout[p, h].wait_recv()
            fb[i] = (wp[i] + opp[i].astype(F32) + rsr[i].astype(F32)).astype(BF16)
            if p == 0:
                ret[h].start()
            else:
                kept_here[h].start()

    blocks = range(4)
    branch(0, multiply(0))

    @pl.when(sec >= 2)
    def _():
        for i in blocks:
            chain(0, i)

    arrivals = multiply(1)

    @pl.when(sec >= 2)
    def _():
        for i in blocks:
            deliver(0, i)

    branch(1, arrivals)
    weights()

    @pl.when(sec >= 2)
    def _():
        for i in blocks:
            chain(1, i)
            deliver(1, i)
        for n in range(4):
            relay(*steps[n])

    @pl.when(sec < 2)
    def _():
        for i in blocks:
            chain(0, i)
            deliver(0, i)
        for n in range(4):
            relay(*steps[n])
            chain(1, n)
            deliver(1, n)

    for step in steps:
        settle(*step)
    for (m, i, e), cp in final.items():
        if i < 3:
            cp.wait_recv()
            cp.wait_send()
        else:
            cp.wait()
    for cp in sends:
        cp.wait_send()

    @pl.when(holds)
    def _():
        for cp in list(wout.values()) + list(ret.values()):
            cp.wait_send()
        for h in range(2):
            kept_here[h].wait()

    @pl.when(lacks)
    def _():
        for cp in wcross + list(rout.values()):
            cp.wait_send()
        for h in range(2):
            ret[h].wait_recv()

    @pl.when(sec > 0)
    def _():
        for cp in chained.values():
            cp.wait_send()


def on_device(layer_inputs, value_cotangent, value_weight, norm_gain, skip_keep, top_grad):
    any_ = pl.BlockSpec(memory_space=pl.ANY)
    dma = pltpu.SemaphoreType.DMA
    sums, weight = pl.pallas_call(
        kernel,
        name="backward",
        out_shape=(
            jax.ShapeDtypeStruct((MB, ROWS, 4096), BF16),
            jax.ShapeDtypeStruct((HALF, HALF), BF16),
        ),
        in_specs=[
            any_, any_, any_,
            pl.BlockSpec(memory_space=pltpu.VMEM),
            pl.BlockSpec(memory_space=pltpu.SMEM),
        ],
        out_specs=(any_, any_),
        scratch_shapes=[
            pltpu.VMEM((MB, ROWS, HALF), BF16),
            pltpu.VMEM((MB, 2, 4, ROWS, HALF), BF16),
            pltpu.VMEM((2, 2, HALF, HALF), BF16),
            pltpu.VMEM((MB, 4, ROWS, SUB), BF16),
            pltpu.VMEM((MB, HALF, SUB), F32),
            pltpu.VMEM((MB, HALF, SUB), BF16),
            pltpu.VMEM((2, HALF, 128), F32),
            pltpu.VMEM((MB, 8, 8, HALF), F32),
            pltpu.VMEM((4, 256, HALF), F32),
            pltpu.VMEM((4, 256, HALF), BF16),
            pltpu.VMEM((4, 256, HALF), BF16),
            pltpu.VMEM((4, 256, HALF), BF16),
            pltpu.VMEM((4, 256, HALF), BF16),
            pltpu.VMEM((4, 256, HALF), BF16),
            pltpu.VMEM((MB, 4, ROWS, SUB), BF16),
            pltpu.VMEM((8, ROWS, SUB), BF16),
            dma((8,)),
            dma((MB,)), dma((MB,)),
            dma((MB, 2, 3)), dma((MB, 2, 3)),
            dma((MB, 3, 2)), dma((MB, 3, 2)),
            dma((2,)), dma((2,)),
            dma((2, 2, 2)), dma((2, 2, 2)),
            dma((MB, 7)), dma((MB, 7)),
            dma((8,)), dma((8,)),
            dma((MB, 3, 2)), dma((MB, 3, 2)),
            dma((4,)), dma((4,)),
            dma((4,)), dma((4,)),
            dma((2,)), dma((2,)),
        ],
        compiler_params=pltpu.CompilerParams(
            collective_id=0, has_side_effects=True, vmem_limit_bytes=56 * 1024 * 1024
        ),
    )(layer_inputs, value_cotangent, value_weight, norm_gain, skip_keep.reshape(1, MB))
    total_rows = MB * ROWS * lax.axis_size("dp")
    factor = float(total_rows) ** (-0.5)
    grads = top_grad.astype(F32) + sums.astype(F32)
    return grads[None], (weight.astype(F32) * factor)[None]


def solution(mesh):
    placed = (
        P("section", None, "dp", None),
        P("section", None, "dp", "tensor"),
        P("section", "dp", "tensor"),
        P("section", None),
        P("section", None, "dp"),
        P(None, "dp", "tensor"),
    )
    return jax.shard_map(
        on_device,
        mesh=mesh,
        in_specs=placed,
        out_specs=(P("section", None, "dp", "tensor"), P("section", "dp", "tensor")),
        check_vma=False,
    )
```

```python
import functools

import jax
import jax.numpy as jnp
from jax import lax
from jax.experimental import pallas as pl
from jax.experimental.pallas import tpu as pltpu
from jax.sharding import PartitionSpec as P

EPSILON = 1e-05
MESH = pl.DeviceIdType.MESH
MB = 2
ROWS = 128
D = 8192
SUB = 1024
HALF = 512
ORDER = (2, 1, 3)
F32 = jnp.float32
BF16 = jnp.bfloat16


def nt(a, b):
    return lax.dot_general(a, b, (((1,), (1,)), ((), ())), preferred_element_type=F32)


def tn(a, b):
    return lax.dot_general(a, b, (((0,), (0,)), ((), ())), preferred_element_type=F32)


def exact(a, b, dims):
    return lax.dot_general(
        a, b, (dims, ((), ())), preferred_element_type=F32, precision=lax.Precision.HIGHEST
    )


def kernel(
    x_hbm, c_hbm, w_hbm, gain, keep,
    s_out, w_out,
    cot, rowx, cg, wg, xg, scaled, normed, acc, invb, coefb, squares, stat, wp, rsi, opp, rso, rsr, fb, sb, ci,
    loc, qs, qr, zs, zr, cs, cr, xs, xr, ps, pr, ws, wr, ts, tr, hs, hr, as_, ar, os_, or_, rs, rr, bs, br,
):
    sec = lax.axis_index("section")
    dp = lax.axis_index("dp")
    t = lax.axis_index("tensor")
    x, y = dp // 4, dp % 4

    def at(nx, ny, ntensor):
        return (sec, nx * 4 + ny, ntensor)

    def yp(k):
        return at(x, (y + k) % 4, t)

    zp = at(x, y, 1 - t)
    odd = x % 2
    holds = (x // 2) == t
    lacks = jnp.logical_not(holds)
    here = holds.astype(jnp.int32) * (2 * odd - 1) + 1 - odd
    inner = at(x + 1 - 2 * odd, y, t)
    outer = at((x + 3 + 2 * odd) % 4, y, t)
    stat_peers = [(k, e) for e in (0, 1) for k in (2, 1, 3, 0) if (k, e) != (0, 0)]
    part = [pl.ds(0, 256), pl.ds(256, 256)]

    def feature(block, ny):
        return pl.multiple_of(t * 4096 + block * 2048 + ny * HALF, HALF)

    def remote(src, dst, ssem, rsem, dev):
        return pltpu.make_async_remote_copy(
            src_ref=src, dst_ref=dst, send_sem=ssem, recv_sem=rsem, device_id=dev,
            device_id_type=MESH,
        )

    own_c = pltpu.make_async_copy(c_hbm.at[0], cot, loc.at[0])
    own_c.start()
    own_w = pltpu.make_async_copy(w_hbm.at[0], wg.at[here, t], loc.at[1])

    @pl.when(holds)
    def _():
        own_w.start()

    own_x = {}
    for m in range(MB):
        for e in range(2):
            own_x[m, e] = pltpu.make_async_copy(
                x_hbm.at[0, m, :, pl.ds(feature(e, y), HALF)],
                xg.at[m, y, :, pl.ds(e * HALF, HALF)],
                loc.at[2 + 2 * m + e],
            )
            own_x[m, e].start()

    own_rows = pltpu.make_async_copy(
        x_hbm.at[0, :, :, pl.ds(pl.multiple_of(t * 4096, 4096), 4096)], rowx, loc.at[8]
    )
    own_rows.start()

    barrier = pltpu.get_barrier_semaphore()
    peers = [at(x, (y + k) % 4, (t + e) % 2) for k, e in stat_peers]
    peers += [inner, outer, ((sec + 1) % 4, dp, t), ((sec + 3) % 4, dp, t)]
    for dev in peers:
        pl.semaphore_signal(barrier, inc=1, device_id=dev, device_id_type=MESH)
    own_c.wait()
    for m in range(MB):
        kept = keep[0, m].astype(F32)
        cg[m, t, y] = (cot[m].astype(F32) * kept).astype(BF16)
    pl.semaphore_wait(barrier, len(peers))

    sends = []

    def go(cp):
        cp.start()
        sends.append(cp)
        return cp

    def send_cot(m, half, i, col, origin, k):
        return go(
            remote(
                cg.at[m, col, origin], cg.at[m, col, origin],
                cs.at[m, half, i], cr.at[m, half, i], yp(k),
            )
        )

    cat = {}
    zc = [
        go(remote(cg.at[m, t, y], cg.at[m, t, y], zs.at[m], zr.at[m], zp)) for m in range(MB)
    ]

    def send_own(m):
        cat[m, 0, 0] = send_cot(m, 0, 0, t, y, 1)
        cat[m, 0, 1] = send_cot(m, 0, 1, t, y, 3)

    def send_other(m):
        zc[m].wait_recv()
        cat[m, 1, 0] = send_cot(m, 1, 0, 1 - t, y, 1)
        cat[m, 1, 1] = send_cot(m, 1, 1, 1 - t, y, 3)

    def pass_own(m):
        wait_cot((m, 0, 0))
        cat[m, 0, 2] = send_cot(m, 0, 2, t, down, 1)

    def pass_other(m):
        wait_cot((m, 1, 1))
        cat[m, 1, 2] = send_cot(m, 1, 2, 1 - t, up, 3)

    up, down = (y + 1) % 4, (y + 3) % 4
    send_own(0)
    got = set()

    def wait_cot(key):
        if key not in got:
            got.add(key)
            cat[key].wait_recv()

    wcross = [
        remote(w_hbm.at[0, part[h]], wg.at[odd, t, part[h]], ps.at[h], pr.at[h], zp)
        for h in range(2)
    ]

    @pl.when(lacks)
    def _():
        for h in range(2):
            wcross[h].start()

    win, wout = {}, {}
    for p in range(2):
        col = t if p == 0 else 1 - t
        for h in range(2):
            block = wg.at[here, col, part[h]]
            win[p, h] = remote(block, block, ws.at[p, h, 0], wr.at[p, h, 0], inner)
            wout[p, h] = remote(block, block, ws.at[p, h, 1], wr.at[p, h, 1], outer)

    def weight_step(p, h):
        @pl.when(holds)
        def _():
            if p == 1:
                wcross[h].wait_recv()
                wout[p, h].start()

        @pl.when(lacks)
        def _():
            wout[p, h].wait_recv()

        go(win[p, h])

    xat = {}

    def send_x(m, h):
        for i, k in enumerate(ORDER):
            for e in range(2):
                start = pl.multiple_of(feature(e, (y + k) % 4) + h * 256, 256)
                xat[m, h, i, e] = go(
                    remote(
                        x_hbm.at[0, m, :, pl.ds(start, 256)],
                        xg.at[m, y, :, pl.ds(e * HALF + h * 256, 256)],
                        xs.at[m, h, i, e], xr.at[m, h, i, e], yp(k),
                    )
                )

    @pl.when(holds)
    def _():
        own_w.wait()
        wout[0, 0].start()
        wout[0, 1].start()

    send_x(0, 0)
    lane_row = lax.broadcasted_iota(jnp.int32, (8, 128), 0)
    ones = jnp.ones((8, 128), F32)
    first_row = jnp.where(lane_row == 0, 1.0, 0.0).astype(F32)
    me = 2 * y + t

    def tell(src, slots, ssem, rsem):
        return [
            go(
                remote(
                    src, slots, ssem.at[i], rsem.at[i], at(x, (y + k) % 4, (t + e) % 2)
                )
            )
            for i, (k, e) in enumerate(stat_peers)
        ]

    own_rows.wait()
    for m in range(MB):

        def square(i, total):
            xf = rowx[m, :, pl.ds(pl.multiple_of(i * 512, 512), 512)].astype(F32)
            xf = xf * xf
            return total + (xf[:, :128] + xf[:, 128:256]) + (xf[:, 256:384] + xf[:, 384:])

        total = lax.fori_loop(0, 8, square, jnp.zeros((ROWS, 128), F32))
        squares[me, :, m * ROWS : (m + 1) * ROWS] = exact(ones, total, ((1,), (1,)))
    sums = tell(squares.at[me], squares.at[me], qs, qr)

    send_other(0)
    pass_own(0)
    send_x(0, 1)
    weight_step(0, 0)
    send_own(1)
    send_other(1)
    pass_other(0)
    weight_step(0, 1)
    pass_own(1)
    send_x(1, 0)
    pass_other(1)
    weight_step(1, 0)
    send_x(1, 1)
    weight_step(1, 1)

    for cp in sums:
        cp.wait_recv()
    for n in range(4):
        total = squares[2 * n] + squares[2 * n + 1]
        inv = lax.rsqrt(total * (1.0 / D) + EPSILON)
        wide = exact(inv, first_row, ((0,), (0,)))
        for m in range(MB):
            invb[m, n] = wide[m * ROWS : (m + 1) * ROWS]

    def multiply(m):
        for half in range(2):
            for i in range(3):
                wait_cot((m, half, i))
        if m == 0:
            for cp in win.values():
                cp.wait_recv()

        def tile(i, carry):
            rows = pl.ds(pl.multiple_of((i % 2) * 256, 256), 256)
            cols = pl.ds(pl.multiple_of(i * 256, 256), 256)
            ng = nt(cg[m, 0].reshape(HALF, HALF), wg[i // 2, 0, rows, :])
            ng += nt(cg[m, 1].reshape(HALF, HALF), wg[i // 2, 1, rows, :])
            start = pl.multiple_of(feature(i // 2, y) + (i % 2) * 256, 256)
            scaled[m, :, cols] = ng * gain[0:1, pl.ds(start, 256)]
            return carry

        lax.fori_loop(0, 4, tile, 0)

    def inputs(m, h):
        if h == 0:
            for e in range(2):
                own_x[m, e].wait()
        for e in range(2):
            for i in range(3):
                xat[m, h, i, e].wait_recv()
        inv = invb[m].reshape(HALF, 128)

        def tile(i, total):
            at_col = pl.multiple_of((i // 2) * HALF + h * 256 + (i % 2) * 128, 128)
            cols = pl.ds(at_col, 128)
            start = pl.multiple_of(feature(i // 2, y) + h * 256 + (i % 2) * 128, 128)
            xf = xg[m, :, :, cols].reshape(HALF, 128).astype(F32)
            normed[m, :, cols] = (xf * inv * gain[0:1, pl.ds(start, 128)]).astype(BF16)
            if h == 0:
                acc[...] = jnp.where(i == 0, 0.0, acc[...]) + xf * scaled[m, :, cols]
            else:
                acc[...] += xf * scaled[m, :, cols]
            return total

        lax.fori_loop(0, 4, tile, 0)

    def share(m):
        stat[m, me] = exact(ones, acc[...], ((1,), (1,)))
        return tell(stat.at[m, me], stat.at[m, me], ts.at[m], tr.at[m])

    def coefficients(m, arrivals):
        for cp in arrivals:
            cp.wait_recv()
        total = jnp.sum(stat[m], axis=0) * (1.0 / D)
        dots = exact(total, first_row, ((0,), (0,)))
        inv = invb[m].reshape(HALF, 128)
        coefb[m] = (inv * inv * inv * dots).reshape(4, ROWS, 128)

    below = (sec - 1, dp, t)
    chained = {}
    final = {}
    spots = (2, 1, 3, 0)
    for m in range(MB):
        for i, k in enumerate(spots):
            yb = (y + k) % 4
            b = m * 4 + i
            chained[m, i] = remote(sb.at[m, yb], ci.at[b], hs.at[b], hr.at[b], below)
            for e in range(2):
                src = sb.at[m, yb, :, pl.ds(e * HALF, HALF)]
                spot = s_out.at[m, :, pl.ds(pl.multiple_of(e * 2048 + y * HALF, HALF), HALF)]
                if k:
                    final[m, i, e] = remote(src, spot, as_.at[m, i, e], ar.at[m, i, e], yp(k))
                else:
                    final[m, i, e] = pltpu.make_async_copy(src, spot, loc.at[2 + 2 * m + e])

    def chain(m, i):
        yb = (y + spots[i]) % 4
        cp = chained[m, i]
        rows = pl.ds(pl.multiple_of(yb * ROWS, ROWS), ROWS)

        def put(above):
            def tile(n, carry):
                cols = pl.ds(pl.multiple_of(n * 128, 128), 128)
                xf = xg[m, yb, :, cols].astype(F32)
                value = invb[m, yb] * scaled[m, rows, cols] - xf * coefb[m, yb]
                if above:
                    value += ci[m * 4 + i, :, cols].astype(F32)
                sb[m, yb, :, cols] = value.astype(BF16)
                return carry

            lax.fori_loop(0, 8, tile, 0)

        @pl.when(sec < 3)
        def _():
            cp.wait_recv()
            put(True)

        @pl.when(sec == 3)
        def _():
            put(False)

        @pl.when(sec > 0)
        def _():
            cp.start()

    def deliver(m, i):
        for e in range(2):
            final[m, i, e].start()

    def product(block, p, h):
        col = 1 - t if p == 0 else t
        cols = pl.ds(pl.multiple_of(block * HALF + h * 256, 256), 256)
        total = tn(normed[0, :, cols], cg[0, col].reshape(HALF, HALF))
        total += tn(normed[1, :, cols], cg[1, col].reshape(HALF, HALF))
        return total

    steps = [(p, h) for h in range(2) for p in range(2)]
    rin, rout, ret, kept_here = {}, {}, {}, {}
    for p, h in steps:
        i = 2 * p + h
        rin[p, h] = remote(rsi.at[i], opp.at[i], rs.at[i], rr.at[i], inner)
        rout[p, h] = remote(rso.at[i], rsr.at[i], os_.at[i], or_.at[i], outer)
    for h in range(2):
        ret[h] = remote(fb.at[h], w_out.at[part[h]], bs.at[h], br.at[h], zp)
        kept_here[h] = pltpu.make_async_copy(fb.at[2 + h], w_out.at[part[h]], loc.at[6 + h])

    def weights(h):
        for p in range(2):
            i = 2 * p + h
            rsi[i] = product(1 - here, p, h).astype(BF16)
            go(rin[p, h])
            wp[i] = product(here, p, h)

    def relay(p, h):
        i = 2 * p + h
        rin[p, h].wait_recv()

        @pl.when(lacks)
        def _():
            rso[i] = (wp[i] + opp[i].astype(F32)).astype(BF16)
            rout[p, h].start()

    def settle(p, h):
        i = 2 * p + h

        @pl.when(holds)
        def _():
            rout[p, h].wait_recv()
            fb[i] = (wp[i] + opp[i].astype(F32) + rsr[i].astype(F32)).astype(BF16)
            if p == 0:
                ret[h].start()
            else:
                kept_here[h].start()

    blocks = range(4)
    multiply(0)
    inputs(0, 0)
    inputs(0, 1)
    arrivals = share(0)
    multiply(1)
    coefficients(0, arrivals)

    @pl.when(sec >= 2)
    def _():
        for i in blocks:
            chain(0, i)

    inputs(1, 0)
    weights(0)
    inputs(1, 1)
    arrivals = share(1)

    @pl.when(sec >= 2)
    def _():
        for i in blocks:
            deliver(0, i)

    weights(1)
    relay(*steps[0])
    coefficients(1, arrivals)

    @pl.when(sec >= 2)
    def _():
        for i in blocks:
            chain(1, i)
            deliver(1, i)
        for n in (1, 2, 3):
            relay(*steps[n])

    @pl.when(sec < 2)
    def _():
        for i in blocks:
            chain(0, i)
            deliver(0, i)
        for n in (1, 2, 3):
            relay(*steps[n])
            chain(1, n - 1)
            deliver(1, n - 1)
        chain(1, 3)
        deliver(1, 3)

    for step in steps:
        settle(*step)
    for (m, i, e), cp in final.items():
        if i < 3:
            cp.wait_recv()
            cp.wait_send()
        else:
            cp.wait()
    for cp in sends:
        cp.wait_send()

    @pl.when(holds)
    def _():
        for cp in list(wout.values()) + list(ret.values()):
            cp.wait_send()
        for h in range(2):
            kept_here[h].wait()

    @pl.when(lacks)
    def _():
        for cp in wcross + list(rout.values()):
            cp.wait_send()
        for h in range(2):
            ret[h].wait_recv()

    @pl.when(sec > 0)
    def _():
        for cp in chained.values():
            cp.wait_send()


def on_device(layer_inputs, value_cotangent, value_weight, norm_gain, skip_keep, top_grad):
    any_ = pl.BlockSpec(memory_space=pl.ANY)
    dma = pltpu.SemaphoreType.DMA
    sums, weight = pl.pallas_call(
        kernel,
        name="backward",
        out_shape=(
            jax.ShapeDtypeStruct((MB, ROWS, 4096), BF16),
            jax.ShapeDtypeStruct((HALF, HALF), BF16),
        ),
        in_specs=[
            any_, any_, any_,
            pl.BlockSpec(memory_space=pltpu.VMEM),
            pl.BlockSpec(memory_space=pltpu.SMEM),
        ],
        out_specs=(any_, any_),
        scratch_shapes=[
            pltpu.VMEM((MB, ROWS, HALF), BF16),
            pltpu.VMEM((MB, ROWS, 4096), BF16),
            pltpu.VMEM((MB, 2, 4, ROWS, HALF), BF16),
            pltpu.VMEM((2, 2, HALF, HALF), BF16),
            pltpu.VMEM((MB, 4, ROWS, SUB), BF16),
            pltpu.VMEM((MB, HALF, SUB), F32),
            pltpu.VMEM((MB, HALF, SUB), BF16),
            pltpu.VMEM((HALF, 128), F32),
            pltpu.VMEM((MB, 4, ROWS, 128), F32),
            pltpu.VMEM((MB, 4, ROWS, 128), F32),
            pltpu.VMEM((8, 8, 2 * ROWS), F32),
            pltpu.VMEM((MB, 8, 8, HALF), F32),
            pltpu.VMEM((4, 256, HALF), F32),
            pltpu.VMEM((4, 256, HALF), BF16),
            pltpu.VMEM((4, 256, HALF), BF16),
            pltpu.VMEM((4, 256, HALF), BF16),
            pltpu.VMEM((4, 256, HALF), BF16),
            pltpu.VMEM((4, 256, HALF), BF16),
            pltpu.VMEM((MB, 4, ROWS, SUB), BF16),
            pltpu.VMEM((8, ROWS, SUB), BF16),
            dma((9,)),
            dma((7,)), dma((7,)),
            dma((MB,)), dma((MB,)),
            dma((MB, 2, 3)), dma((MB, 2, 3)),
            dma((MB, 2, 3, 2)), dma((MB, 2, 3, 2)),
            dma((2,)), dma((2,)),
            dma((2, 2, 2)), dma((2, 2, 2)),
            dma((MB, 7)), dma((MB, 7)),
            dma((8,)), dma((8,)),
            dma((MB, 3, 2)), dma((MB, 3, 2)),
            dma((4,)), dma((4,)),
            dma((4,)), dma((4,)),
            dma((2,)), dma((2,)),
        ],
        compiler_params=pltpu.CompilerParams(
            collective_id=0, has_side_effects=True, vmem_limit_bytes=56 * 1024 * 1024
        ),
    )(layer_inputs, value_cotangent, value_weight, norm_gain, skip_keep.reshape(1, MB))
    total_rows = MB * ROWS * lax.axis_size("dp")
    factor = float(total_rows) ** (-0.5)
    grads = top_grad.astype(F32) + sums.astype(F32)
    return grads[None], (weight.astype(F32) * factor)[None]


def solution(mesh):
    placed = (
        P("section", None, "dp", None),
        P("section", None, "dp", "tensor"),
        P("section", "dp", "tensor"),
        P("section", None),
        P("section", None, "dp"),
        P(None, "dp", "tensor"),
    )
    return jax.shard_map(
        on_device,
        mesh=mesh,
        in_specs=placed,
        out_specs=(P("section", None, "dp", "tensor"), P("section", "dp", "tensor")),
        check_vma=False,
    )
```

```python
import functools

import jax
import jax.numpy as jnp
from jax import lax
from jax.experimental import pallas as pl
from jax.experimental.pallas import tpu as pltpu
from jax.sharding import PartitionSpec as P

EPSILON = 1e-05
MESH = pl.DeviceIdType.MESH
MB = 2
ROWS = 128
D = 8192
SUB = 1024
HALF = 512
ORDER = (2, 1, 3)
F32 = jnp.float32
BF16 = jnp.bfloat16


def nt(a, b):
    return lax.dot_general(a, b, (((1,), (1,)), ((), ())), preferred_element_type=F32)


def tn(a, b):
    return lax.dot_general(a, b, (((0,), (0,)), ((), ())), preferred_element_type=F32)


def exact(a, b, dims):
    return lax.dot_general(
        a, b, (dims, ((), ())), preferred_element_type=F32, precision=lax.Precision.HIGHEST
    )


def kernel(
    x_hbm, c_hbm, w_hbm, gain, keep,
    s_out, w_out,
    cot, rowx, cg, wg, xg, scaled, normed, acc, invb, coefb, squares, stat, wp, rsi, opp, rso, rsr, fb, sb, ci,
    loc, qs, qr, zs, zr, cs, cr, xs, xr, ps, pr, ws, wr, ts, tr, hs, hr, as_, ar, os_, or_, rs, rr, bs, br,
):
    sec = lax.axis_index("section")
    dp = lax.axis_index("dp")
    t = lax.axis_index("tensor")
    x, y = dp // 4, dp % 4

    def at(nx, ny, ntensor):
        return (sec, nx * 4 + ny, ntensor)

    def yp(k):
        return at(x, (y + k) % 4, t)

    zp = at(x, y, 1 - t)
    odd = x % 2
    holds = (x // 2) == t
    lacks = jnp.logical_not(holds)
    here = holds.astype(jnp.int32) * (2 * odd - 1) + 1 - odd
    inner = at(x + 1 - 2 * odd, y, t)
    outer = at((x + 3 + 2 * odd) % 4, y, t)
    stat_peers = [(k, e) for e in (0, 1) for k in (2, 1, 3, 0) if (k, e) != (0, 0)]
    part = [pl.ds(0, 256), pl.ds(256, 256)]

    def feature(block, ny):
        return pl.multiple_of(t * 4096 + block * 2048 + ny * HALF, HALF)

    def remote(src, dst, ssem, rsem, dev):
        return pltpu.make_async_remote_copy(
            src_ref=src, dst_ref=dst, send_sem=ssem, recv_sem=rsem, device_id=dev,
            device_id_type=MESH,
        )

    own_c = pltpu.make_async_copy(c_hbm.at[0], cot, loc.at[0])
    own_c.start()
    own_w = pltpu.make_async_copy(w_hbm.at[0], wg.at[here, t], loc.at[1])

    @pl.when(holds)
    def _():
        own_w.start()

    own_x = {}
    for m in range(MB):
        for e in range(2):
            own_x[m, e] = pltpu.make_async_copy(
                x_hbm.at[0, m, :, pl.ds(feature(e, y), HALF)],
                xg.at[m, y, :, pl.ds(e * HALF, HALF)],
                loc.at[2 + 2 * m + e],
            )
            own_x[m, e].start()

    own_rows = pltpu.make_async_copy(
        x_hbm.at[0, :, :, pl.ds(pl.multiple_of(t * 4096, 4096), 4096)], rowx, loc.at[8]
    )
    own_rows.start()

    barrier = pltpu.get_barrier_semaphore()
    peers = [at(x, (y + k) % 4, (t + e) % 2) for k, e in stat_peers]
    peers += [inner, outer, ((sec + 1) % 4, dp, t), ((sec + 3) % 4, dp, t)]
    for dev in peers:
        pl.semaphore_signal(barrier, inc=1, device_id=dev, device_id_type=MESH)
    own_c.wait()
    for m in range(MB):
        kept = keep[0, m].astype(F32)
        cg[m, t, y] = (cot[m].astype(F32) * kept).astype(BF16)
    pl.semaphore_wait(barrier, len(peers))

    sends = []

    def go(cp):
        cp.start()
        sends.append(cp)
        return cp

    def send_cot(m, half, i, col, origin, k):
        return go(
            remote(
                cg.at[m, col, origin], cg.at[m, col, origin],
                cs.at[m, half, i], cr.at[m, half, i], yp(k),
            )
        )

    cat = {}
    zc = {}

    def send_z(m):
        zc[m] = go(remote(cg.at[m, t, y], cg.at[m, t, y], zs.at[m], zr.at[m], zp))

    def send_own(m):
        cat[m, 0, 0] = send_cot(m, 0, 0, t, y, 1)
        cat[m, 0, 1] = send_cot(m, 0, 1, t, y, 3)

    def send_other(m):
        zc[m].wait_recv()
        cat[m, 1, 0] = send_cot(m, 1, 0, 1 - t, y, 1)
        cat[m, 1, 1] = send_cot(m, 1, 1, 1 - t, y, 3)

    def pass_own(m):
        wait_cot((m, 0, 0))
        cat[m, 0, 2] = send_cot(m, 0, 2, t, down, 1)

    def pass_other(m):
        wait_cot((m, 1, 1))
        cat[m, 1, 2] = send_cot(m, 1, 2, 1 - t, up, 3)

    up, down = (y + 1) % 4, (y + 3) % 4
    got = set()

    def wait_cot(key):
        if key not in got:
            got.add(key)
            cat[key].wait_recv()

    pieces = [(p, 128 * n, 128) for p in range(2) for n in range(4)]
    wcross, win, wout = {}, {}, {}
    for n, (p, first, size) in enumerate(pieces):
        rows = pl.ds(first, size)
        if p:
            wcross[n] = remote(
                w_hbm.at[0, rows], wg.at[odd, t, rows], ps.at[n], pr.at[n], zp
            )
        block = wg.at[here, 1 - t if p else t, rows]
        win[n] = remote(block, block, ws.at[n, 0], wr.at[n, 0], inner)
        wout[n] = remote(block, block, ws.at[n, 1], wr.at[n, 1], outer)

    def weight_step(n):
        if n in wcross:
            @pl.when(holds)
            def _():
                wcross[n].wait_recv()
                wout[n].start()
                win[n].start()

        @pl.when(lacks)
        def _():
            wout[n].wait_recv()
            win[n].start()

    xat = {}

    def send_x(m, h):
        for i, k in enumerate(ORDER):
            for e in range(2):
                start = pl.multiple_of(feature(e, (y + k) % 4) + h * 256, 256)
                xat[m, h, i, e] = go(
                    remote(
                        x_hbm.at[0, m, :, pl.ds(start, 256)],
                        xg.at[m, y, :, pl.ds(e * HALF + h * 256, 256)],
                        xs.at[m, h, i, e], xr.at[m, h, i, e], yp(k),
                    )
                )

    @pl.when(holds)
    def _():
        own_w.wait()
        for n in range(4):
            wout[n].start()
            win[n].start()

    for m in range(MB):
        send_z(m)
        send_own(m)

    @pl.when(lacks)
    def _():
        for cp in wcross.values():
            cp.start()

    lane_row = lax.broadcasted_iota(jnp.int32, (8, 128), 0)
    ones = jnp.ones((8, 128), F32)
    first_row = jnp.where(lane_row == 0, 1.0, 0.0).astype(F32)
    me = 2 * y + t

    def tell(src, slots, ssem, rsem):
        return [
            go(
                remote(
                    src, slots, ssem.at[i], rsem.at[i], at(x, (y + k) % 4, (t + e) % 2)
                )
            )
            for i, (k, e) in enumerate(stat_peers)
        ]

    own_rows.wait()
    for m in range(MB):

        def square(i, total):
            xf = rowx[m, :, pl.ds(pl.multiple_of(i * 512, 512), 512)].astype(F32)
            xf = xf * xf
            return total + (xf[:, :128] + xf[:, 128:256]) + (xf[:, 256:384] + xf[:, 384:])

        total = lax.fori_loop(0, 8, square, jnp.zeros((ROWS, 128), F32))
        squares[me, :, m * ROWS : (m + 1) * ROWS] = exact(ones, total, ((1,), (1,)))
    sums = tell(squares.at[me], squares.at[me], qs, qr)

    weight_step(0)
    send_other(0)
    pass_own(0)
    weight_step(1)
    send_other(1)
    pass_own(1)
    send_x(0, 0)
    weight_step(2)
    weight_step(3)
    pass_other(0)
    send_x(0, 1)
    weight_step(4)
    pass_other(1)
    send_x(1, 0)
    weight_step(5)
    weight_step(6)
    weight_step(7)
    send_x(1, 1)

    for cp in sums:
        cp.wait_recv()
    for n in range(4):
        total = squares[2 * n] + squares[2 * n + 1]
        inv = lax.rsqrt(total * (1.0 / D) + EPSILON)
        wide = exact(inv, first_row, ((0,), (0,)))
        for m in range(MB):
            invb[m, n] = wide[m * ROWS : (m + 1) * ROWS]

    def cotangent(m):
        for half in range(2):
            for i in range(3):
                wait_cot((m, half, i))

    def multiply(m):
        if m == 0:
            for cp in win.values():
                cp.wait_recv()

        def tile(i, carry):
            rows = pl.ds(pl.multiple_of((i % 2) * 256, 256), 256)
            cols = pl.ds(pl.multiple_of(i * 256, 256), 256)
            ng = nt(cg[m, 0].reshape(HALF, HALF), wg[i // 2, 0, rows, :])
            ng += nt(cg[m, 1].reshape(HALF, HALF), wg[i // 2, 1, rows, :])
            start = pl.multiple_of(feature(i // 2, y) + (i % 2) * 256, 256)
            scaled[m, :, cols] = ng * gain[0:1, pl.ds(start, 256)]
            return carry

        lax.fori_loop(0, 4, tile, 0)

    def inputs(m, h):
        if h == 0:
            for e in range(2):
                own_x[m, e].wait()
        for e in range(2):
            for i in range(3):
                xat[m, h, i, e].wait_recv()
        inv = invb[m].reshape(HALF, 128)

        def tile(i, carry):
            at_col = pl.multiple_of((i // 2) * HALF + h * 256 + (i % 2) * 128, 128)
            cols = pl.ds(at_col, 128)
            start = pl.multiple_of(feature(i // 2, y) + h * 256 + (i % 2) * 128, 128)
            xf = xg[m, :, :, cols].reshape(HALF, 128).astype(F32)
            normed[m, :, cols] = (xf * inv * gain[0:1, pl.ds(start, 128)]).astype(BF16)
            return carry

        lax.fori_loop(0, 4, tile, 0)

    def dots(m):
        acc[...] = jnp.zeros_like(acc)

        def tile(i, carry):
            cols = pl.ds(pl.multiple_of(i * 128, 128), 128)
            xf = xg[m, :, :, cols].reshape(HALF, 128).astype(F32)
            acc[...] += xf * scaled[m, :, cols]
            return carry

        lax.fori_loop(0, 8, tile, 0)

    def share(m):
        stat[m, me] = exact(ones, acc[...], ((1,), (1,)))
        return tell(stat.at[m, me], stat.at[m, me], ts.at[m], tr.at[m])

    def coefficients(m, arrivals):
        for cp in arrivals:
            cp.wait_recv()
        total = jnp.sum(stat[m], axis=0) * (1.0 / D)
        wide = exact(total, first_row, ((0,), (0,)))
        inv = invb[m].reshape(HALF, 128)
        coefb[m] = (inv * inv * inv * wide).reshape(4, ROWS, 128)

    below = (sec - 1, dp, t)
    chained = {}
    final = {}
    spots = (2, 1, 3, 0)
    for m in range(MB):
        for i, k in enumerate(spots):
            yb = (y + k) % 4
            b = m * 4 + i
            chained[m, i] = remote(sb.at[m, yb], ci.at[b], hs.at[b], hr.at[b], below)
            for e in range(2):
                src = sb.at[m, yb, :, pl.ds(e * HALF, HALF)]
                spot = s_out.at[m, :, pl.ds(pl.multiple_of(e * 2048 + y * HALF, HALF), HALF)]
                if k:
                    final[m, i, e] = remote(src, spot, as_.at[m, i, e], ar.at[m, i, e], yp(k))
                else:
                    final[m, i, e] = pltpu.make_async_copy(src, spot, loc.at[2 + 2 * m + e])

    def chain(m, i):
        yb = (y + spots[i]) % 4
        cp = chained[m, i]
        rows = pl.ds(pl.multiple_of(yb * ROWS, ROWS), ROWS)

        def put(above):
            def tile(n, carry):
                cols = pl.ds(pl.multiple_of(n * 128, 128), 128)
                xf = xg[m, yb, :, cols].astype(F32)
                value = invb[m, yb] * scaled[m, rows, cols] - xf * coefb[m, yb]
                if above:
                    value += ci[m * 4 + i, :, cols].astype(F32)
                sb[m, yb, :, cols] = value.astype(BF16)
                return carry

            lax.fori_loop(0, 8, tile, 0)

        @pl.when(sec < 3)
        def _():
            cp.wait_recv()
            put(True)

        @pl.when(sec == 3)
        def _():
            put(False)

        @pl.when(sec > 0)
        def _():
            cp.start()

    def deliver(m, i):
        for e in range(2):
            final[m, i, e].start()

    def product(block, p, h):
        col = 1 - t if p == 0 else t
        cols = pl.ds(pl.multiple_of(block * HALF + h * 256, 256), 256)
        total = tn(normed[0, :, cols], cg[0, col].reshape(HALF, HALF))
        total += tn(normed[1, :, cols], cg[1, col].reshape(HALF, HALF))
        return total

    steps = [(p, h) for h in range(2) for p in range(2)]
    rin, rout, ret, kept_here = {}, {}, {}, {}
    for p, h in steps:
        i = 2 * p + h
        rin[p, h] = remote(rsi.at[i], opp.at[i], rs.at[i], rr.at[i], inner)
        rout[p, h] = remote(rso.at[i], rsr.at[i], os_.at[i], or_.at[i], outer)
    for h in range(2):
        ret[h] = remote(fb.at[h], w_out.at[part[h]], bs.at[h], br.at[h], zp)
        kept_here[h] = pltpu.make_async_copy(fb.at[2 + h], w_out.at[part[h]], loc.at[6 + h])

    def weights(h):
        for p in range(2):
            i = 2 * p + h
            rsi[i] = product(1 - here, p, h).astype(BF16)
            go(rin[p, h])
            wp[i] = product(here, p, h)

    def relay(p, h):
        i = 2 * p + h
        rin[p, h].wait_recv()

        @pl.when(lacks)
        def _():
            rso[i] = (wp[i] + opp[i].astype(F32)).astype(BF16)
            rout[p, h].start()

    def settle(p, h):
        i = 2 * p + h

        @pl.when(holds)
        def _():
            rout[p, h].wait_recv()
            fb[i] = (wp[i] + opp[i].astype(F32) + rsr[i].astype(F32)).astype(BF16)
            if p == 0:
                ret[h].start()
            else:
                kept_here[h].start()

    blocks = range(4)

    def block(m, i):
        chain(m, i)
        deliver(m, i)

    cotangent(0)
    multiply(0)
    inputs(0, 0)
    inputs(0, 1)
    dots(0)
    arrivals = share(0)
    cotangent(1)
    multiply(1)
    coefficients(0, arrivals)

    @pl.when(sec >= 2)
    def _():
        for i in blocks:
            chain(0, i)

    inputs(1, 0)
    weights(0)
    inputs(1, 1)
    dots(1)
    arrivals = share(1)
    weights(1)
    relay(*steps[0])
    coefficients(1, arrivals)

    @pl.when(sec >= 2)
    def _():
        for i in blocks:
            chain(1, i)
        for m in range(MB):
            for i in blocks:
                deliver(m, i)
        relay(*steps[1])
        settle(*steps[0])
        relay(*steps[2])
        settle(*steps[1])
        relay(*steps[3])
        settle(*steps[2])
        settle(*steps[3])

    @pl.when(sec < 2)
    def _():
        for i in blocks:
            block(0, i)
        relay(*steps[1])
        settle(*steps[0])
        block(1, 0)
        relay(*steps[2])
        settle(*steps[1])
        block(1, 1)
        block(1, 2)
        relay(*steps[3])
        settle(*steps[2])
        block(1, 3)
        settle(*steps[3])

    for (m, i, e), cp in final.items():
        if i < 3:
            cp.wait_recv()
            cp.wait_send()
        else:
            cp.wait()
    for cp in sends + list(win.values()):
        cp.wait_send()

    @pl.when(holds)
    def _():
        for cp in list(wout.values()) + list(ret.values()):
            cp.wait_send()
        for h in range(2):
            kept_here[h].wait()

    @pl.when(lacks)
    def _():
        for cp in list(wcross.values()) + list(rout.values()):
            cp.wait_send()
        for h in range(2):
            ret[h].wait_recv()

    @pl.when(sec > 0)
    def _():
        for cp in chained.values():
            cp.wait_send()


def on_device(layer_inputs, value_cotangent, value_weight, norm_gain, skip_keep, top_grad):
    any_ = pl.BlockSpec(memory_space=pl.ANY)
    dma = pltpu.SemaphoreType.DMA
    sums, weight = pl.pallas_call(
        kernel,
        name="backward",
        out_shape=(
            jax.ShapeDtypeStruct((MB, ROWS, 4096), BF16),
            jax.ShapeDtypeStruct((HALF, HALF), BF16),
        ),
        in_specs=[
            any_, any_, any_,
            pl.BlockSpec(memory_space=pltpu.VMEM),
            pl.BlockSpec(memory_space=pltpu.SMEM),
        ],
        out_specs=(any_, any_),
        scratch_shapes=[
            pltpu.VMEM((MB, ROWS, HALF), BF16),
            pltpu.VMEM((MB, ROWS, 4096), BF16),
            pltpu.VMEM((MB, 2, 4, ROWS, HALF), BF16),
            pltpu.VMEM((2, 2, HALF, HALF), BF16),
            pltpu.VMEM((MB, 4, ROWS, SUB), BF16),
            pltpu.VMEM((MB, HALF, SUB), F32),
            pltpu.VMEM((MB, HALF, SUB), BF16),
            pltpu.VMEM((HALF, 128), F32),
            pltpu.VMEM((MB, 4, ROWS, 128), F32),
            pltpu.VMEM((MB, 4, ROWS, 128), F32),
            pltpu.VMEM((8, 8, 2 * ROWS), F32),
            pltpu.VMEM((MB, 8, 8, HALF), F32),
            pltpu.VMEM((4, 256, HALF), F32),
            pltpu.VMEM((4, 256, HALF), BF16),
            pltpu.VMEM((4, 256, HALF), BF16),
            pltpu.VMEM((4, 256, HALF), BF16),
            pltpu.VMEM((4, 256, HALF), BF16),
            pltpu.VMEM((4, 256, HALF), BF16),
            pltpu.VMEM((MB, 4, ROWS, SUB), BF16),
            pltpu.VMEM((8, ROWS, SUB), BF16),
            dma((9,)),
            dma((7,)), dma((7,)),
            dma((MB,)), dma((MB,)),
            dma((MB, 2, 3)), dma((MB, 2, 3)),
            dma((MB, 2, 3, 2)), dma((MB, 2, 3, 2)),
            dma((8,)), dma((8,)),
            dma((8, 2)), dma((8, 2)),
            dma((MB, 7)), dma((MB, 7)),
            dma((8,)), dma((8,)),
            dma((MB, 3, 2)), dma((MB, 3, 2)),
            dma((4,)), dma((4,)),
            dma((4,)), dma((4,)),
            dma((2,)), dma((2,)),
        ],
        compiler_params=pltpu.CompilerParams(
            collective_id=0, has_side_effects=True, vmem_limit_bytes=56 * 1024 * 1024
        ),
    )(layer_inputs, value_cotangent, value_weight, norm_gain, skip_keep.reshape(1, MB))
    total_rows = MB * ROWS * lax.axis_size("dp")
    factor = float(total_rows) ** (-0.5)
    grads = top_grad.astype(F32) + sums.astype(F32)
    return grads[None], (weight.astype(F32) * factor)[None]


def solution(mesh):
    placed = (
        P("section", None, "dp", None),
        P("section", None, "dp", "tensor"),
        P("section", "dp", "tensor"),
        P("section", None),
        P("section", None, "dp"),
        P(None, "dp", "tensor"),
    )
    return jax.shard_map(
        on_device,
        mesh=mesh,
        in_specs=placed,
        out_specs=(P("section", None, "dp", "tensor"), P("section", "dp", "tensor")),
        check_vma=False,
    )
```

```python
import functools

import jax
import jax.numpy as jnp
from jax import lax
from jax.experimental import pallas as pl
from jax.experimental.pallas import tpu as pltpu
from jax.sharding import PartitionSpec as P

EPSILON = 1e-05
MESH = pl.DeviceIdType.MESH
MB = 2
ROWS = 128
D = 8192
SUB = 1024
HALF = 512
ORDER = (2, 1, 3)
F32 = jnp.float32
BF16 = jnp.bfloat16


def nt(a, b):
    return lax.dot_general(a, b, (((1,), (1,)), ((), ())), preferred_element_type=F32)


def tn(a, b):
    return lax.dot_general(a, b, (((0,), (0,)), ((), ())), preferred_element_type=F32)


def exact(a, b, dims):
    return lax.dot_general(
        a, b, (dims, ((), ())), preferred_element_type=F32, precision=lax.Precision.HIGHEST
    )


def kernel(
    x_hbm, c_hbm, w_hbm, gain, keep,
    s_out, w_out,
    cot, rowx, cg, wg, xg, scaled, normed, acc, invb, coefb, squares, stat, wp, rsi, opp, rso, rsr, fb, sb, ci, via,
    loc, qs, qr, zs, zr, cs, cr, xs, xr, ps, pr, ws, wr, ts, tr, hs, hr, vs, vr, as_, ar, os_, or_, rs, rr, bs, br,
):
    sec = lax.axis_index("section")
    dp = lax.axis_index("dp")
    t = lax.axis_index("tensor")
    x, y = dp // 4, dp % 4

    def at(nx, ny, ntensor):
        return (sec, nx * 4 + ny, ntensor)

    def yp(k):
        return at(x, (y + k) % 4, t)

    zp = at(x, y, 1 - t)
    odd = x % 2
    holds = (x // 2) == t
    lacks = jnp.logical_not(holds)
    here = holds.astype(jnp.int32) * (2 * odd - 1) + 1 - odd
    inner = at(x + 1 - 2 * odd, y, t)
    outer = at((x + 3 + 2 * odd) % 4, y, t)
    stat_peers = [(k, e) for e in (0, 1) for k in (2, 1, 3, 0) if (k, e) != (0, 0)]
    part = [pl.ds(0, 256), pl.ds(256, 256)]

    def feature(block, ny):
        return pl.multiple_of(t * 4096 + block * 2048 + ny * HALF, HALF)

    def remote(src, dst, ssem, rsem, dev):
        return pltpu.make_async_remote_copy(
            src_ref=src, dst_ref=dst, send_sem=ssem, recv_sem=rsem, device_id=dev,
            device_id_type=MESH,
        )

    own_c = pltpu.make_async_copy(c_hbm.at[0], cot, loc.at[0])
    own_c.start()
    own_w = pltpu.make_async_copy(w_hbm.at[0], wg.at[here, t], loc.at[1])

    @pl.when(holds)
    def _():
        own_w.start()

    own_x = {}
    for m in range(MB):
        for e in range(2):
            own_x[m, e] = pltpu.make_async_copy(
                x_hbm.at[0, m, :, pl.ds(feature(e, y), HALF)],
                xg.at[m, y, :, pl.ds(e * HALF, HALF)],
                loc.at[2 + 2 * m + e],
            )
            own_x[m, e].start()

    own_rows = pltpu.make_async_copy(
        x_hbm.at[0, :, :, pl.ds(pl.multiple_of(t * 4096, 4096), 4096)], rowx, loc.at[8]
    )
    own_rows.start()

    barrier = pltpu.get_barrier_semaphore()
    peers = [at(x, (y + k) % 4, (t + e) % 2) for k, e in stat_peers]
    peers += [inner, outer, ((sec + 1) % 4, dp, t), ((sec + 3) % 4, dp, t)]
    peers += [((sec + 2) % 4, dp, 1 - t)]
    for dev in peers:
        pl.semaphore_signal(barrier, inc=1, device_id=dev, device_id_type=MESH)
    own_c.wait()
    for m in range(MB):
        kept = keep[0, m].astype(F32)
        cg[m, t, y] = (cot[m].astype(F32) * kept).astype(BF16)
    pl.semaphore_wait(barrier, len(peers))

    sends = []

    def go(cp):
        cp.start()
        sends.append(cp)
        return cp

    def send_cot(m, half, i, col, origin, k):
        return go(
            remote(
                cg.at[m, col, origin], cg.at[m, col, origin],
                cs.at[m, half, i], cr.at[m, half, i], yp(k),
            )
        )

    cat = {}
    zc = {}

    def send_z(m):
        zc[m] = go(remote(cg.at[m, t, y], cg.at[m, t, y], zs.at[m], zr.at[m], zp))

    def send_own(m):
        cat[m, 0, 0] = send_cot(m, 0, 0, t, y, 1)
        cat[m, 0, 1] = send_cot(m, 0, 1, t, y, 3)

    def send_other(m):
        zc[m].wait_recv()
        cat[m, 1, 0] = send_cot(m, 1, 0, 1 - t, y, 1)
        cat[m, 1, 1] = send_cot(m, 1, 1, 1 - t, y, 3)

    def pass_own(m):
        wait_cot((m, 0, 0))
        cat[m, 0, 2] = send_cot(m, 0, 2, t, down, 1)

    def pass_other(m):
        wait_cot((m, 1, 1))
        cat[m, 1, 2] = send_cot(m, 1, 2, 1 - t, up, 3)

    up, down = (y + 1) % 4, (y + 3) % 4
    got = set()

    def wait_cot(key):
        if key not in got:
            got.add(key)
            cat[key].wait_recv()

    pieces = [(p, 128 * n, 128) for p in range(2) for n in range(4)]
    wcross, win, wout = {}, {}, {}
    for n, (p, first, size) in enumerate(pieces):
        rows = pl.ds(first, size)
        if p:
            wcross[n] = remote(
                w_hbm.at[0, rows], wg.at[odd, t, rows], ps.at[n], pr.at[n], zp
            )
        block = wg.at[here, 1 - t if p else t, rows]
        win[n] = remote(block, block, ws.at[n, 0], wr.at[n, 0], inner)
        wout[n] = remote(block, block, ws.at[n, 1], wr.at[n, 1], outer)

    def weight_step(n):
        if n in wcross:
            @pl.when(holds)
            def _():
                wcross[n].wait_recv()
                wout[n].start()
                win[n].start()

        @pl.when(lacks)
        def _():
            wout[n].wait_recv()
            win[n].start()

    xat = {}

    def send_x(m, h):
        for i, k in enumerate(ORDER):
            for e in range(2):
                start = pl.multiple_of(feature(e, (y + k) % 4) + h * 256, 256)
                xat[m, h, i, e] = go(
                    remote(
                        x_hbm.at[0, m, :, pl.ds(start, 256)],
                        xg.at[m, y, :, pl.ds(e * HALF + h * 256, 256)],
                        xs.at[m, h, i, e], xr.at[m, h, i, e], yp(k),
                    )
                )

    @pl.when(holds)
    def _():
        own_w.wait()
        for n in range(4):
            wout[n].start()
            win[n].start()

    for m in range(MB):
        send_z(m)
        send_own(m)

    @pl.when(lacks)
    def _():
        for cp in wcross.values():
            cp.start()

    lane_row = lax.broadcasted_iota(jnp.int32, (8, 128), 0)
    ones = jnp.ones((8, 128), F32)
    first_row = jnp.where(lane_row == 0, 1.0, 0.0).astype(F32)
    me = 2 * y + t

    def tell(src, slots, ssem, rsem):
        return [
            go(
                remote(
                    src, slots, ssem.at[i], rsem.at[i], at(x, (y + k) % 4, (t + e) % 2)
                )
            )
            for i, (k, e) in enumerate(stat_peers)
        ]

    own_rows.wait()
    for m in range(MB):

        def square(i, total):
            xf = rowx[m, :, pl.ds(pl.multiple_of(i * 512, 512), 512)].astype(F32)
            xf = xf * xf
            return total + (xf[:, :128] + xf[:, 128:256]) + (xf[:, 256:384] + xf[:, 384:])

        total = lax.fori_loop(0, 8, square, jnp.zeros((ROWS, 128), F32))
        squares[me, :, m * ROWS : (m + 1) * ROWS] = exact(ones, total, ((1,), (1,)))
    sums = tell(squares.at[me], squares.at[me], qs, qr)

    weight_step(0)
    send_other(0)
    pass_own(0)
    weight_step(1)
    send_other(1)
    pass_own(1)
    send_x(0, 0)
    weight_step(2)
    weight_step(3)
    pass_other(0)
    send_x(0, 1)
    weight_step(4)
    pass_other(1)
    send_x(1, 0)
    weight_step(5)
    weight_step(6)
    weight_step(7)

    for cp in sums:
        cp.wait_recv()
    for n in range(4):
        total = squares[2 * n] + squares[2 * n + 1]
        inv = lax.rsqrt(total * (1.0 / D) + EPSILON)
        wide = exact(inv, first_row, ((0,), (0,)))
        for m in range(MB):
            invb[m, n] = wide[m * ROWS : (m + 1) * ROWS]

    def cotangent(m):
        for half in range(2):
            for i in range(3):
                wait_cot((m, half, i))

    def multiply(m):
        if m == 0:
            for cp in win.values():
                cp.wait_recv()

        def tile(i, carry):
            rows = pl.ds(pl.multiple_of((i % 2) * 256, 256), 256)
            cols = pl.ds(pl.multiple_of(i * 256, 256), 256)
            ng = nt(cg[m, 0].reshape(HALF, HALF), wg[i // 2, 0, rows, :])
            ng += nt(cg[m, 1].reshape(HALF, HALF), wg[i // 2, 1, rows, :])
            start = pl.multiple_of(feature(i // 2, y) + (i % 2) * 256, 256)
            scaled[m, :, cols] = ng * gain[0:1, pl.ds(start, 256)]
            return carry

        lax.fori_loop(0, 4, tile, 0)

    def inputs(m, h):
        if h == 0:
            for e in range(2):
                own_x[m, e].wait()
        for e in range(2):
            for i in range(3):
                xat[m, h, i, e].wait_recv()
        inv = invb[m].reshape(HALF, 128)

        def tile(i, carry):
            at_col = pl.multiple_of((i // 2) * HALF + h * 256 + (i % 2) * 128, 128)
            cols = pl.ds(at_col, 128)
            start = pl.multiple_of(feature(i // 2, y) + h * 256 + (i % 2) * 128, 128)
            xf = xg[m, :, :, cols].reshape(HALF, 128).astype(F32)
            normed[m, :, cols] = (xf * inv * gain[0:1, pl.ds(start, 128)]).astype(BF16)
            return carry

        lax.fori_loop(0, 4, tile, 0)

    def dots(m):
        acc[...] = jnp.zeros_like(acc)

        def tile(i, carry):
            cols = pl.ds(pl.multiple_of(i * 128, 128), 128)
            xf = xg[m, :, :, cols].reshape(HALF, 128).astype(F32)
            acc[...] += xf * scaled[m, :, cols]
            return carry

        lax.fori_loop(0, 8, tile, 0)

    def share(m):
        stat[m, me] = exact(ones, acc[...], ((1,), (1,)))
        return tell(stat.at[m, me], stat.at[m, me], ts.at[m], tr.at[m])

    def coefficients(m, arrivals):
        for cp in arrivals:
            cp.wait_recv()
        total = jnp.sum(stat[m], axis=0) * (1.0 / D)
        wide = exact(total, first_row, ((0,), (0,)))
        inv = invb[m].reshape(HALF, 128)
        coefb[m] = (inv * inv * inv * wide).reshape(4, ROWS, 128)

    below = (sec - 1, dp, t)
    chained = {}
    final = {}
    spots = (2, 1, 3, 0)
    for m in range(MB):
        for i, k in enumerate(spots):
            yb = (y + k) % 4
            b = m * 4 + i
            chained[m, i] = remote(sb.at[m, yb], ci.at[b], hs.at[b], hr.at[b], below)
            for e in range(2):
                src = sb.at[m, yb, :, pl.ds(e * HALF, HALF)]
                spot = s_out.at[m, :, pl.ds(pl.multiple_of(e * 2048 + y * HALF, HALF), HALF)]
                if k:
                    final[m, i, e] = remote(src, spot, as_.at[m, i, e], ar.at[m, i, e], yp(k))
                else:
                    final[m, i, e] = pltpu.make_async_copy(src, spot, loc.at[2 + 2 * m + e])

    hops = {}
    for m in range(MB):
        yb = (y + spots[3]) % 4
        hops[m, 0] = remote(sb.at[m, yb], via.at[m, 0], vs.at[m, 0], vr.at[m, 0], (0, dp, 1 - t))
        hops[m, 1] = remote(via.at[m, 0], via.at[m, 1], vs.at[m, 1], vr.at[m, 1], (3, dp, t))
        hops[m, 2] = remote(
            via.at[m, 1], ci.at[m * 4 + 3], vs.at[m, 2], hr.at[m * 4 + 3], (1, dp, 1 - t)
        )

    def forward(m, n):
        @pl.when(sec == (0 if n == 0 else 3))
        def _():
            hops[m, n].wait_recv()
            hops[m, n + 1].start()

    def chain(m, i):
        yb = (y + spots[i]) % 4
        cp = chained[m, i]
        rows = pl.ds(pl.multiple_of(yb * ROWS, ROWS), ROWS)

        def put(above):
            def tile(n, carry):
                cols = pl.ds(pl.multiple_of(n * 128, 128), 128)
                xf = xg[m, yb, :, cols].astype(F32)
                value = invb[m, yb] * scaled[m, rows, cols] - xf * coefb[m, yb]
                if above:
                    value += ci[m * 4 + i, :, cols].astype(F32)
                sb[m, yb, :, cols] = value.astype(BF16)
                return carry

            lax.fori_loop(0, 8, tile, 0)

        @pl.when(sec < 3)
        def _():
            cp.wait_recv()
            put(True)

        @pl.when(sec == 3)
        def _():
            put(False)

        if i == 3:
            @pl.when(sec % 2 == 1)
            def _():
                cp.start()

            @pl.when(sec == 2)
            def _():
                hops[m, 0].start()

        else:
            @pl.when(sec > 0)
            def _():
                cp.start()

    def deliver(m, i):
        for e in range(2):
            final[m, i, e].start()

    def product(block, p, h):
        col = 1 - t if p == 0 else t
        cols = pl.ds(pl.multiple_of(block * HALF + h * 256, 256), 256)
        total = tn(normed[0, :, cols], cg[0, col].reshape(HALF, HALF))
        total += tn(normed[1, :, cols], cg[1, col].reshape(HALF, HALF))
        return total

    steps = [(p, h) for h in range(2) for p in range(2)]
    rin, rout, ret, kept_here = {}, {}, {}, {}
    for p, h in steps:
        i = 2 * p + h
        rin[p, h] = remote(rsi.at[i], opp.at[i], rs.at[i], rr.at[i], inner)
        rout[p, h] = remote(rso.at[i], rsr.at[i], os_.at[i], or_.at[i], outer)
    for h in range(2):
        ret[h] = remote(fb.at[h], w_out.at[part[h]], bs.at[h], br.at[h], zp)
        kept_here[h] = pltpu.make_async_copy(fb.at[2 + h], w_out.at[part[h]], loc.at[6 + h])

    def weights(h):
        for p in range(2):
            i = 2 * p + h
            rsi[i] = product(1 - here, p, h).astype(BF16)
            go(rin[p, h])
            wp[i] = product(here, p, h)

    def relay(p, h):
        i = 2 * p + h
        rin[p, h].wait_recv()

        @pl.when(lacks)
        def _():
            rso[i] = (wp[i] + opp[i].astype(F32)).astype(BF16)
            rout[p, h].start()

    def settle(p, h):
        i = 2 * p + h

        @pl.when(holds)
        def _():
            rout[p, h].wait_recv()
            fb[i] = (wp[i] + opp[i].astype(F32) + rsr[i].astype(F32)).astype(BF16)
            if p == 0:
                ret[h].start()
            else:
                kept_here[h].start()

    blocks = range(4)

    def block(m, i):
        chain(m, i)
        deliver(m, i)

    cotangent(0)
    multiply(0)
    inputs(0, 0)
    inputs(0, 1)
    dots(0)
    arrivals = share(0)
    send_x(1, 1)
    cotangent(1)
    inputs(1, 0)
    weights(0)
    coefficients(0, arrivals)

    @pl.when(sec >= 2)
    def _():
        for i in (3, 0, 1, 2):
            chain(0, i)

    multiply(1)
    inputs(1, 1)
    dots(1)
    arrivals = share(1)
    weights(1)
    relay(*steps[0])

    @pl.when(sec >= 2)
    def _():
        for i in blocks:
            deliver(0, i)

    @pl.when(sec < 2)
    def _():
        forward(0, 0)
        block(0, 0)
        block(0, 1)

    coefficients(1, arrivals)

    @pl.when(sec >= 2)
    def _():
        for i in (3, 0, 1, 2):
            chain(1, i)
            deliver(1, i)
        forward(0, 1)
        relay(*steps[1])
        settle(*steps[0])
        relay(*steps[2])
        settle(*steps[1])
        forward(1, 1)
        relay(*steps[3])
        settle(*steps[2])
        settle(*steps[3])

    @pl.when(sec < 2)
    def _():
        relay(*steps[1])
        block(0, 2)
        forward(1, 0)
        settle(*steps[0])
        block(0, 3)
        relay(*steps[2])
        settle(*steps[1])
        block(1, 0)
        block(1, 1)
        relay(*steps[3])
        settle(*steps[2])
        block(1, 2)
        block(1, 3)
        settle(*steps[3])

    for (m, i, e), cp in final.items():
        if i < 3:
            cp.wait_recv()
            cp.wait_send()
        else:
            cp.wait()
    for cp in sends + list(win.values()):
        cp.wait_send()

    @pl.when(holds)
    def _():
        for cp in list(wout.values()) + list(ret.values()):
            cp.wait_send()
        for h in range(2):
            kept_here[h].wait()

    @pl.when(lacks)
    def _():
        for cp in list(wcross.values()) + list(rout.values()):
            cp.wait_send()
        for h in range(2):
            ret[h].wait_recv()

    @pl.when(sec > 0)
    def _():
        for (m, i), cp in chained.items():
            if i < 3:
                cp.wait_send()

    for n, sender in enumerate((2, 0, 3)):

        @pl.when(sec == sender)
        def _():
            for m in range(MB):
                hops[m, n].wait_send()

    @pl.when(sec % 2 == 1)
    def _():
        for m in range(MB):
            chained[m, 3].wait_send()


def finish(factor, top, sums, weight, grads, scaled):
    grads[...] = top[...].astype(F32) + sums[...].astype(F32)
    scaled[...] = weight[...].astype(F32) * factor


def on_device(layer_inputs, value_cotangent, value_weight, norm_gain, skip_keep, top_grad):
    any_ = pl.BlockSpec(memory_space=pl.ANY)
    dma = pltpu.SemaphoreType.DMA
    sums, weight = pl.pallas_call(
        kernel,
        name="backward",
        out_shape=(
            jax.ShapeDtypeStruct((MB, ROWS, 4096), BF16),
            jax.ShapeDtypeStruct((HALF, HALF), BF16),
        ),
        in_specs=[
            any_, any_, any_,
            pl.BlockSpec(memory_space=pltpu.VMEM),
            pl.BlockSpec(memory_space=pltpu.SMEM),
        ],
        out_specs=(any_, any_),
        scratch_shapes=[
            pltpu.VMEM((MB, ROWS, HALF), BF16),
            pltpu.VMEM((MB, ROWS, 4096), BF16),
            pltpu.VMEM((MB, 2, 4, ROWS, HALF), BF16),
            pltpu.VMEM((2, 2, HALF, HALF), BF16),
            pltpu.VMEM((MB, 4, ROWS, SUB), BF16),
            pltpu.VMEM((MB, HALF, SUB), F32),
            pltpu.VMEM((MB, HALF, SUB), BF16),
            pltpu.VMEM((HALF, 128), F32),
            pltpu.VMEM((MB, 4, ROWS, 128), F32),
            pltpu.VMEM((MB, 4, ROWS, 128), F32),
            pltpu.VMEM((8, 8, 2 * ROWS), F32),
            pltpu.VMEM((MB, 8, 8, HALF), F32),
            pltpu.VMEM((4, 256, HALF), F32),
            pltpu.VMEM((4, 256, HALF), BF16),
            pltpu.VMEM((4, 256, HALF), BF16),
            pltpu.VMEM((4, 256, HALF), BF16),
            pltpu.VMEM((4, 256, HALF), BF16),
            pltpu.VMEM((4, 256, HALF), BF16),
            pltpu.VMEM((MB, 4, ROWS, SUB), BF16),
            pltpu.VMEM((8, ROWS, SUB), BF16),
            pltpu.VMEM((MB, 2, ROWS, SUB), BF16),
            dma((9,)),
            dma((7,)), dma((7,)),
            dma((MB,)), dma((MB,)),
            dma((MB, 2, 3)), dma((MB, 2, 3)),
            dma((MB, 2, 3, 2)), dma((MB, 2, 3, 2)),
            dma((8,)), dma((8,)),
            dma((8, 2)), dma((8, 2)),
            dma((MB, 7)), dma((MB, 7)),
            dma((8,)), dma((8,)),
            dma((MB, 3)), dma((MB, 2)),
            dma((MB, 3, 2)), dma((MB, 3, 2)),
            dma((4,)), dma((4,)),
            dma((4,)), dma((4,)),
            dma((2,)), dma((2,)),
        ],
        compiler_params=pltpu.CompilerParams(
            collective_id=0, has_side_effects=True, vmem_limit_bytes=56 * 1024 * 1024
        ),
    )(layer_inputs, value_cotangent, value_weight, norm_gain, skip_keep.reshape(1, MB))
    total_rows = MB * ROWS * lax.axis_size("dp")
    factor = float(total_rows) ** (-0.5)
    rows, cols = MB * ROWS // 4, HALF // 4
    grads, scaled = pl.pallas_call(
        functools.partial(finish, factor),
        name="finish",
        out_shape=(
            jax.ShapeDtypeStruct((MB * ROWS, 4096), F32),
            jax.ShapeDtypeStruct((HALF, HALF), F32),
        ),
        grid=(4,),
        in_specs=[
            pl.BlockSpec((rows, 4096), lambda i: (i, 0)),
            pl.BlockSpec((rows, 4096), lambda i: (i, 0)),
            pl.BlockSpec((cols, HALF), lambda i: (i, 0)),
        ],
        out_specs=(
            pl.BlockSpec((rows, 4096), lambda i: (i, 0)),
            pl.BlockSpec((cols, HALF), lambda i: (i, 0)),
        ),
    )(top_grad.reshape(MB * ROWS, 4096), sums.reshape(MB * ROWS, 4096), weight)
    return grads.reshape(1, MB, ROWS, 4096), scaled[None]


def solution(mesh):
    placed = (
        P("section", None, "dp", None),
        P("section", None, "dp", "tensor"),
        P("section", "dp", "tensor"),
        P("section", None),
        P("section", None, "dp"),
        P(None, "dp", "tensor"),
    )
    return jax.shard_map(
        on_device,
        mesh=mesh,
        in_specs=placed,
        out_specs=(P("section", None, "dp", "tensor"), P("section", "dp", "tensor")),
        check_vma=False,
    )
```

```python
import functools

import jax
import jax.numpy as jnp
from jax import lax
from jax.experimental import pallas as pl
from jax.experimental.pallas import tpu as pltpu
from jax.sharding import PartitionSpec as P

EPSILON = 1e-05
MESH = pl.DeviceIdType.MESH
MB = 2
ROWS = 128
D = 8192
SUB = 1024
HALF = 512
ORDER = (2, 1, 3)
F32 = jnp.float32
BF16 = jnp.bfloat16


def nt(a, b):
    return lax.dot_general(a, b, (((1,), (1,)), ((), ())), preferred_element_type=F32)


def tn(a, b):
    return lax.dot_general(a, b, (((0,), (0,)), ((), ())), preferred_element_type=F32)


def exact(a, b, dims):
    return lax.dot_general(
        a, b, (dims, ((), ())), preferred_element_type=F32, precision=lax.Precision.HIGHEST
    )


def kernel(
    x_hbm, c_hbm, w_hbm, gain, keep,
    s_out, w_out,
    cot, rowx, cg, wg, xg, scaled, normed, acc, invb, coefb, squares, stat, wp, rsi, opp, rso, rsr, fb, sb, ci, via,
    loc, qs, qr, zs, zr, cs, cr, xs, xr, ps, pr, ws, wr, ts, tr, hs, hr, vs, vr, as_, ar, os_, or_, rs, rr, bs, br,
):
    sec = lax.axis_index("section")
    dp = lax.axis_index("dp")
    t = lax.axis_index("tensor")
    x, y = dp // 4, dp % 4

    def at(nx, ny, ntensor):
        return (sec, nx * 4 + ny, ntensor)

    def yp(k):
        return at(x, (y + k) % 4, t)

    zp = at(x, y, 1 - t)
    odd = x % 2
    holds = (x // 2) == t
    lacks = jnp.logical_not(holds)
    here = holds.astype(jnp.int32) * (2 * odd - 1) + 1 - odd
    inner = at(x + 1 - 2 * odd, y, t)
    outer = at((x + 3 + 2 * odd) % 4, y, t)
    stat_peers = [(k, e) for e in (0, 1) for k in (2, 1, 3, 0) if (k, e) != (0, 0)]
    part = [pl.ds(0, 256), pl.ds(256, 256)]

    def feature(block, ny):
        return pl.multiple_of(t * 4096 + block * 2048 + ny * HALF, HALF)

    def remote(src, dst, ssem, rsem, dev):
        return pltpu.make_async_remote_copy(
            src_ref=src, dst_ref=dst, send_sem=ssem, recv_sem=rsem, device_id=dev,
            device_id_type=MESH,
        )

    own_c = pltpu.make_async_copy(c_hbm.at[0], cot, loc.at[0])
    own_c.start()
    own_w = pltpu.make_async_copy(w_hbm.at[0], wg.at[here, t], loc.at[1])

    @pl.when(holds)
    def _():
        own_w.start()

    own_x = {}
    for m in range(MB):
        for e in range(2):
            own_x[m, e] = pltpu.make_async_copy(
                x_hbm.at[0, m, :, pl.ds(feature(e, y), HALF)],
                xg.at[m, y, :, pl.ds(e * HALF, HALF)],
                loc.at[2 + 2 * m + e],
            )
            own_x[m, e].start()

    own_rows = pltpu.make_async_copy(
        x_hbm.at[0, :, :, pl.ds(pl.multiple_of(t * 4096, 4096), 4096)], rowx, loc.at[8]
    )
    own_rows.start()

    barrier = pltpu.get_barrier_semaphore()
    peers = [at(x, (y + k) % 4, (t + e) % 2) for k, e in stat_peers]
    peers += [inner, outer, ((sec + 1) % 4, dp, t), ((sec + 3) % 4, dp, t)]
    peers += [((sec + 2) % 4, dp, 1 - t)]
    for dev in peers:
        pl.semaphore_signal(barrier, inc=1, device_id=dev, device_id_type=MESH)
    own_c.wait()
    for m in range(MB):
        kept = keep[0, m].astype(F32)
        cg[m, t, y] = (cot[m].astype(F32) * kept).astype(BF16)
    pl.semaphore_wait(barrier, len(peers))

    sends = []

    def go(cp):
        cp.start()
        sends.append(cp)
        return cp

    def send_cot(m, half, i, col, origin, k):
        return go(
            remote(
                cg.at[m, col, origin], cg.at[m, col, origin],
                cs.at[m, half, i], cr.at[m, half, i], yp(k),
            )
        )

    cat = {}
    zc = {}

    def send_z(m):
        zc[m] = go(remote(cg.at[m, t, y], cg.at[m, t, y], zs.at[m], zr.at[m], zp))

    def send_own(m):
        cat[m, 0, 0] = send_cot(m, 0, 0, t, y, 1)
        cat[m, 0, 1] = send_cot(m, 0, 1, t, y, 3)

    def send_other(m):
        zc[m].wait_recv()
        cat[m, 1, 0] = send_cot(m, 1, 0, 1 - t, y, 1)
        cat[m, 1, 1] = send_cot(m, 1, 1, 1 - t, y, 3)

    def pass_own(m):
        wait_cot((m, 0, 0))
        cat[m, 0, 2] = send_cot(m, 0, 2, t, down, 1)

    def pass_other(m):
        wait_cot((m, 1, 1))
        cat[m, 1, 2] = send_cot(m, 1, 2, 1 - t, up, 3)

    up, down = (y + 1) % 4, (y + 3) % 4
    got = set()

    def wait_cot(key):
        if key not in got:
            got.add(key)
            cat[key].wait_recv()

    pieces = [(p, 128 * n, 128) for p in range(2) for n in range(4)]
    wcross, win, wout = {}, {}, {}
    for n, (p, first, size) in enumerate(pieces):
        rows = pl.ds(first, size)
        if p:
            wcross[n] = remote(
                w_hbm.at[0, rows], wg.at[odd, t, rows], ps.at[n], pr.at[n], zp
            )
        block = wg.at[here, 1 - t if p else t, rows]
        win[n] = remote(block, block, ws.at[n, 0], wr.at[n, 0], inner)
        wout[n] = remote(block, block, ws.at[n, 1], wr.at[n, 1], outer)

    def weight_step(n):
        if n in wcross:
            @pl.when(holds)
            def _():
                wcross[n].wait_recv()
                wout[n].start()
                win[n].start()

        @pl.when(lacks)
        def _():
            wout[n].wait_recv()
            win[n].start()

    xat = {}

    def send_x(m, h):
        for i, k in enumerate(ORDER):
            for e in range(2):
                start = pl.multiple_of(feature(e, (y + k) % 4) + h * 256, 256)
                xat[m, h, i, e] = go(
                    remote(
                        x_hbm.at[0, m, :, pl.ds(start, 256)],
                        xg.at[m, y, :, pl.ds(e * HALF + h * 256, 256)],
                        xs.at[m, h, i, e], xr.at[m, h, i, e], yp(k),
                    )
                )

    @pl.when(holds)
    def _():
        own_w.wait()
        for n in range(4):
            wout[n].start()
            win[n].start()

    for m in range(MB):
        send_z(m)
        send_own(m)

    @pl.when(lacks)
    def _():
        for cp in wcross.values():
            cp.start()

    lane_row = lax.broadcasted_iota(jnp.int32, (8, 128), 0)
    ones = jnp.ones((8, 128), F32)
    first_row = jnp.where(lane_row == 0, 1.0, 0.0).astype(F32)
    me = 2 * y + t

    def tell(src, slots, ssem, rsem):
        return [
            go(
                remote(
                    src, slots, ssem.at[i], rsem.at[i], at(x, (y + k) % 4, (t + e) % 2)
                )
            )
            for i, (k, e) in enumerate(stat_peers)
        ]

    own_rows.wait()
    for m in range(MB):

        def square(i, total):
            xf = rowx[m, :, pl.ds(pl.multiple_of(i * 512, 512), 512)].astype(F32)
            xf = xf * xf
            return total + (xf[:, :128] + xf[:, 128:256]) + (xf[:, 256:384] + xf[:, 384:])

        total = lax.fori_loop(0, 8, square, jnp.zeros((ROWS, 128), F32))
        squares[me, :, m * ROWS : (m + 1) * ROWS] = exact(ones, total, ((1,), (1,)))
    sums = tell(squares.at[me], squares.at[me], qs, qr)

    weight_step(0)
    send_other(0)
    pass_own(0)
    weight_step(1)
    send_other(1)
    pass_own(1)
    send_x(0, 0)
    weight_step(2)
    weight_step(3)
    pass_other(0)
    send_x(0, 1)
    weight_step(4)
    pass_other(1)
    send_x(1, 0)
    weight_step(5)
    weight_step(6)
    weight_step(7)

    for cp in sums:
        cp.wait_recv()
    for n in range(4):
        total = squares[2 * n] + squares[2 * n + 1]
        inv = lax.rsqrt(total * (1.0 / D) + EPSILON)
        wide = exact(inv, first_row, ((0,), (0,)))
        for m in range(MB):
            invb[m, n] = wide[m * ROWS : (m + 1) * ROWS]

    def cotangent(m):
        for half in range(2):
            for i in range(3):
                wait_cot((m, half, i))

    def multiply(m, h):
        if m == 0:
            for n in (0, 1, 4, 5):
                win[n + 2 * h].wait_recv()

        def tile(e, carry):
            rows = pl.ds(h * 256, 256)
            cols = pl.ds(pl.multiple_of(e * HALF + h * 256, 256), 256)
            ng = nt(cg[m, 0].reshape(HALF, HALF), wg[e, 0, rows, :])
            ng += nt(cg[m, 1].reshape(HALF, HALF), wg[e, 1, rows, :])
            start = pl.multiple_of(feature(e, y) + h * 256, 256)
            scaled[m, :, cols] = ng * gain[0:1, pl.ds(start, 256)]
            return carry

        lax.fori_loop(0, 2, tile, 0)

    def inputs(m, h):
        if h == 0:
            for e in range(2):
                own_x[m, e].wait()
        for e in range(2):
            for i in range(3):
                xat[m, h, i, e].wait_recv()
        inv = invb[m].reshape(HALF, 128)

        def tile(i, carry):
            at_col = pl.multiple_of((i // 2) * HALF + h * 256 + (i % 2) * 128, 128)
            cols = pl.ds(at_col, 128)
            start = pl.multiple_of(feature(i // 2, y) + h * 256 + (i % 2) * 128, 128)
            xf = xg[m, :, :, cols].reshape(HALF, 128).astype(F32)
            normed[m, :, cols] = (xf * inv * gain[0:1, pl.ds(start, 128)]).astype(BF16)
            return carry

        lax.fori_loop(0, 4, tile, 0)

    def dots(m, h):
        if h == 0:
            acc[...] = jnp.zeros_like(acc)

        def tile(i, carry):
            at_col = pl.multiple_of((i // 2) * HALF + h * 256 + (i % 2) * 128, 128)
            cols = pl.ds(at_col, 128)
            xf = xg[m, :, :, cols].reshape(HALF, 128).astype(F32)
            acc[...] += xf * scaled[m, :, cols]
            return carry

        lax.fori_loop(0, 4, tile, 0)

    def share(m):
        stat[m, me] = exact(ones, acc[...], ((1,), (1,)))
        return tell(stat.at[m, me], stat.at[m, me], ts.at[m], tr.at[m])

    def coefficients(m, arrivals):
        for cp in arrivals:
            cp.wait_recv()
        total = jnp.sum(stat[m], axis=0) * (1.0 / D)
        wide = exact(total, first_row, ((0,), (0,)))
        inv = invb[m].reshape(HALF, 128)
        coefb[m] = (inv * inv * inv * wide).reshape(4, ROWS, 128)

    below = ((sec + 3) % 4, dp, t)
    chained = {}
    final = {}
    spots = (2, 1, 3, 0)
    for m in range(MB):
        for i, k in enumerate(spots):
            yb = (y + k) % 4
            b = m * 4 + i
            chained[m, i] = remote(sb.at[m, yb], ci.at[b], hs.at[b], hr.at[b], below)
            for e in range(2):
                src = sb.at[m, yb, :, pl.ds(e * HALF, HALF)]
                spot = s_out.at[m, :, pl.ds(pl.multiple_of(e * 2048 + y * HALF, HALF), HALF)]
                if k:
                    final[m, i, e] = remote(src, spot, as_.at[m, i, e], ar.at[m, i, e], yp(k))
                else:
                    final[m, i, e] = pltpu.make_async_copy(src, spot, loc.at[2 + 2 * m + e])

    hops = {}
    for m in range(MB):
        yb = (y + spots[3]) % 4
        hops[m, 0] = remote(sb.at[m, yb], via.at[m, 0], vs.at[m, 0], vr.at[m, 0], (0, dp, 1 - t))
        hops[m, 1] = remote(via.at[m, 0], via.at[m, 1], vs.at[m, 1], vr.at[m, 1], (3, dp, t))
        hops[m, 2] = remote(
            via.at[m, 1], ci.at[m * 4 + 3], vs.at[m, 2], hr.at[m * 4 + 3], (1, dp, 1 - t)
        )

    def forward(m, n):
        @pl.when(sec == (0 if n == 0 else 3))
        def _():
            hops[m, n].wait_recv()
            hops[m, n + 1].start()

    def chain(m, i):
        yb = (y + spots[i]) % 4
        cp = chained[m, i]
        rows = pl.ds(pl.multiple_of(yb * ROWS, ROWS), ROWS)

        def put(above):
            def tile(n, carry):
                cols = pl.ds(pl.multiple_of(n * 128, 128), 128)
                xf = xg[m, yb, :, cols].astype(F32)
                value = invb[m, yb] * scaled[m, rows, cols] - xf * coefb[m, yb]
                if above:
                    value += ci[m * 4 + i, :, cols].astype(F32)
                sb[m, yb, :, cols] = value.astype(BF16)
                return carry

            lax.fori_loop(0, 8, tile, 0)

        @pl.when(sec < 3)
        def _():
            cp.wait_recv()
            put(True)

        @pl.when(sec == 3)
        def _():
            put(False)

        if i == 3:
            @pl.when(sec % 2 == 1)
            def _():
                cp.start()

            @pl.when(sec == 2)
            def _():
                hops[m, 0].start()

        else:
            @pl.when(sec > 0)
            def _():
                cp.start()

    def deliver(m, i):
        for e in range(2):
            final[m, i, e].start()

    def product(block, p, h):
        col = 1 - t if p == 0 else t
        cols = pl.ds(pl.multiple_of(block * HALF + h * 256, 256), 256)
        total = tn(normed[0, :, cols], cg[0, col].reshape(HALF, HALF))
        total += tn(normed[1, :, cols], cg[1, col].reshape(HALF, HALF))
        return total

    steps = [(p, h) for h in range(2) for p in range(2)]
    rin, rout, ret, kept_here = {}, {}, {}, {}
    for p, h in steps:
        i = 2 * p + h
        rin[p, h] = remote(rsi.at[i], opp.at[i], rs.at[i], rr.at[i], inner)
        rout[p, h] = remote(rso.at[i], rsr.at[i], os_.at[i], or_.at[i], outer)
    for h in range(2):
        ret[h] = remote(fb.at[h], w_out.at[part[h]], bs.at[h], br.at[h], zp)
        kept_here[h] = pltpu.make_async_copy(fb.at[2 + h], w_out.at[part[h]], loc.at[6 + h])

    def weights(h):
        for p in range(2):
            i = 2 * p + h
            rsi[i] = product(1 - here, p, h).astype(BF16)
            go(rin[p, h])
            wp[i] = product(here, p, h)

    def relay(p, h):
        i = 2 * p + h
        rin[p, h].wait_recv()

        @pl.when(lacks)
        def _():
            rso[i] = (wp[i] + opp[i].astype(F32)).astype(BF16)
            rout[p, h].start()

    def settle(p, h):
        i = 2 * p + h

        @pl.when(holds)
        def _():
            rout[p, h].wait_recv()
            fb[i] = (wp[i] + opp[i].astype(F32) + rsr[i].astype(F32)).astype(BF16)
            if p == 0:
                ret[h].start()
            else:
                kept_here[h].start()

    blocks = range(4)

    def block(m, i):
        chain(m, i)
        deliver(m, i)

    cotangent(0)
    multiply(0, 0)
    inputs(0, 0)
    dots(0, 0)
    inputs(0, 1)
    multiply(0, 1)
    dots(0, 1)
    arrivals = share(0)
    send_x(1, 1)
    cotangent(1)
    inputs(1, 0)
    weights(0)
    coefficients(0, arrivals)

    @pl.when(sec >= 2)
    def _():
        for i in (3, 0, 1, 2):
            chain(0, i)

    multiply(1, 0)
    multiply(1, 1)
    dots(1, 0)
    inputs(1, 1)
    dots(1, 1)
    arrivals = share(1)
    weights(1)
    relay(*steps[0])

    @pl.when(sec >= 2)
    def _():
        for i in blocks:
            deliver(0, i)

    @pl.when(sec < 2)
    def _():
        forward(0, 0)
        block(0, 0)
        block(0, 1)

    coefficients(1, arrivals)

    @pl.when(sec >= 2)
    def _():
        for i in (3, 0, 1, 2):
            chain(1, i)
            deliver(1, i)
        forward(0, 1)
        relay(*steps[1])
        settle(*steps[0])
        relay(*steps[2])
        settle(*steps[1])
        forward(1, 1)
        relay(*steps[3])
        settle(*steps[2])
        settle(*steps[3])

    @pl.when(sec < 2)
    def _():
        relay(*steps[1])
        block(0, 2)
        forward(1, 0)
        settle(*steps[0])
        block(0, 3)
        relay(*steps[2])
        settle(*steps[1])
        block(1, 0)
        block(1, 1)
        relay(*steps[3])
        settle(*steps[2])
        block(1, 2)
        block(1, 3)
        settle(*steps[3])

    for (m, i, e), cp in final.items():
        if i < 3:
            cp.wait_recv()
            cp.wait_send()
        else:
            cp.wait()
    for cp in sends + list(win.values()):
        cp.wait_send()

    @pl.when(holds)
    def _():
        for cp in list(wout.values()) + list(ret.values()):
            cp.wait_send()
        for h in range(2):
            kept_here[h].wait()

    @pl.when(lacks)
    def _():
        for cp in list(wcross.values()) + list(rout.values()):
            cp.wait_send()
        for h in range(2):
            ret[h].wait_recv()

    @pl.when(sec > 0)
    def _():
        for (m, i), cp in chained.items():
            if i < 3:
                cp.wait_send()

    for n, sender in enumerate((2, 0, 3)):

        @pl.when(sec == sender)
        def _():
            for m in range(MB):
                hops[m, n].wait_send()

    @pl.when(sec % 2 == 1)
    def _():
        for m in range(MB):
            chained[m, 3].wait_send()


def finish(factor, top, sums, weight, grads, scaled):
    grads[...] = top[...].astype(F32) + sums[...].astype(F32)
    scaled[...] = weight[...].astype(F32) * factor


def on_device(layer_inputs, value_cotangent, value_weight, norm_gain, skip_keep, top_grad):
    any_ = pl.BlockSpec(memory_space=pl.ANY)
    dma = pltpu.SemaphoreType.DMA
    sums, weight = pl.pallas_call(
        kernel,
        name="backward",
        out_shape=(
            jax.ShapeDtypeStruct((MB, ROWS, 4096), BF16),
            jax.ShapeDtypeStruct((HALF, HALF), BF16),
        ),
        in_specs=[
            any_, any_, any_,
            pl.BlockSpec(memory_space=pltpu.VMEM),
            pl.BlockSpec(memory_space=pltpu.SMEM),
        ],
        out_specs=(any_, any_),
        scratch_shapes=[
            pltpu.VMEM((MB, ROWS, HALF), BF16),
            pltpu.VMEM((MB, ROWS, 4096), BF16),
            pltpu.VMEM((MB, 2, 4, ROWS, HALF), BF16),
            pltpu.VMEM((2, 2, HALF, HALF), BF16),
            pltpu.VMEM((MB, 4, ROWS, SUB), BF16),
            pltpu.VMEM((MB, HALF, SUB), F32),
            pltpu.VMEM((MB, HALF, SUB), BF16),
            pltpu.VMEM((HALF, 128), F32),
            pltpu.VMEM((MB, 4, ROWS, 128), F32),
            pltpu.VMEM((MB, 4, ROWS, 128), F32),
            pltpu.VMEM((8, 8, 2 * ROWS), F32),
            pltpu.VMEM((MB, 8, 8, HALF), F32),
            pltpu.VMEM((4, 256, HALF), F32),
            pltpu.VMEM((4, 256, HALF), BF16),
            pltpu.VMEM((4, 256, HALF), BF16),
            pltpu.VMEM((4, 256, HALF), BF16),
            pltpu.VMEM((4, 256, HALF), BF16),
            pltpu.VMEM((4, 256, HALF), BF16),
            pltpu.VMEM((MB, 4, ROWS, SUB), BF16),
            pltpu.VMEM((8, ROWS, SUB), BF16),
            pltpu.VMEM((MB, 2, ROWS, SUB), BF16),
            dma((9,)),
            dma((7,)), dma((7,)),
            dma((MB,)), dma((MB,)),
            dma((MB, 2, 3)), dma((MB, 2, 3)),
            dma((MB, 2, 3, 2)), dma((MB, 2, 3, 2)),
            dma((8,)), dma((8,)),
            dma((8, 2)), dma((8, 2)),
            dma((MB, 7)), dma((MB, 7)),
            dma((8,)), dma((8,)),
            dma((MB, 3)), dma((MB, 2)),
            dma((MB, 3, 2)), dma((MB, 3, 2)),
            dma((4,)), dma((4,)),
            dma((4,)), dma((4,)),
            dma((2,)), dma((2,)),
        ],
        compiler_params=pltpu.CompilerParams(
            collective_id=0, has_side_effects=True, vmem_limit_bytes=56 * 1024 * 1024
        ),
    )(layer_inputs, value_cotangent, value_weight, norm_gain, skip_keep.reshape(1, MB))
    total_rows = MB * ROWS * lax.axis_size("dp")
    factor = float(total_rows) ** (-0.5)
    rows, cols = MB * ROWS // 4, HALF // 4
    grads, scaled = pl.pallas_call(
        functools.partial(finish, factor),
        name="finish",
        out_shape=(
            jax.ShapeDtypeStruct((MB * ROWS, 4096), F32),
            jax.ShapeDtypeStruct((HALF, HALF), F32),
        ),
        grid=(4,),
        in_specs=[
            pl.BlockSpec((rows, 4096), lambda i: (i, 0)),
            pl.BlockSpec((rows, 4096), lambda i: (i, 0)),
            pl.BlockSpec((cols, HALF), lambda i: (i, 0)),
        ],
        out_specs=(
            pl.BlockSpec((rows, 4096), lambda i: (i, 0)),
            pl.BlockSpec((cols, HALF), lambda i: (i, 0)),
        ),
    )(top_grad.reshape(MB * ROWS, 4096), sums.reshape(MB * ROWS, 4096), weight)
    return grads.reshape(1, MB, ROWS, 4096), scaled[None]


def solution(mesh):
    placed = (
        P("section", None, "dp", None),
        P("section", None, "dp", "tensor"),
        P("section", "dp", "tensor"),
        P("section", None),
        P("section", None, "dp"),
        P(None, "dp", "tensor"),
    )
    return jax.shard_map(
        on_device,
        mesh=mesh,
        in_specs=placed,
        out_specs=(P("section", None, "dp", "tensor"), P("section", "dp", "tensor")),
        check_vma=False,
    )
```

```python
import functools

import jax
import jax.numpy as jnp
from jax import lax
from jax.experimental import pallas as pl
from jax.experimental.pallas import tpu as pltpu
from jax.sharding import PartitionSpec as P

EPSILON = 1e-05
MESH = pl.DeviceIdType.MESH
MB = 2
ROWS = 128
D = 8192
SUB = 1024
HALF = 512
ORDER = (2, 1, 3)
F32 = jnp.float32
BF16 = jnp.bfloat16


def nt(a, b):
    return lax.dot_general(a, b, (((1,), (1,)), ((), ())), preferred_element_type=F32)


def tn(a, b):
    return lax.dot_general(a, b, (((0,), (0,)), ((), ())), preferred_element_type=F32)


def exact(a, b, dims):
    return lax.dot_general(
        a, b, (dims, ((), ())), preferred_element_type=F32, precision=lax.Precision.HIGHEST
    )


def kernel(
    x_hbm, c_hbm, w_hbm, gain, keep,
    s_out, w_out,
    cot, rowx, cg, wg, xg, scaled, normed, acc, invb, coefb, squares, stat, wp, rsi, opp, rso, rsr, fb, sb, ci, via,
    loc, qs, qr, zs, zr, cs, cr, xs, xr, ps, pr, ws, wr, ts, tr, hs, hr, vs, vr, as_, ar, os_, or_, rs, rr, bs, br,
):
    sec = lax.axis_index("section")
    dp = lax.axis_index("dp")
    t = lax.axis_index("tensor")
    x, y = dp // 4, dp % 4

    def at(nx, ny, ntensor):
        return (sec, nx * 4 + ny, ntensor)

    def yp(k):
        return at(x, (y + k) % 4, t)

    zp = at(x, y, 1 - t)
    odd = x % 2
    holds = (x // 2) == t
    lacks = jnp.logical_not(holds)
    here = holds.astype(jnp.int32) * (2 * odd - 1) + 1 - odd
    inner = at(x + 1 - 2 * odd, y, t)
    outer = at((x + 3 + 2 * odd) % 4, y, t)
    stat_peers = [(k, e) for e in (0, 1) for k in (2, 1, 3, 0) if (k, e) != (0, 0)]
    part = [pl.ds(0, 256), pl.ds(256, 256)]

    def feature(block, ny):
        return pl.multiple_of(t * 4096 + block * 2048 + ny * HALF, HALF)

    def remote(src, dst, ssem, rsem, dev):
        return pltpu.make_async_remote_copy(
            src_ref=src, dst_ref=dst, send_sem=ssem, recv_sem=rsem, device_id=dev,
            device_id_type=MESH,
        )

    own_c = pltpu.make_async_copy(c_hbm.at[0], cot, loc.at[0])
    own_c.start()
    own_w = pltpu.make_async_copy(w_hbm.at[0], wg.at[here, t], loc.at[1])

    @pl.when(holds)
    def _():
        own_w.start()

    own_x = {}
    for m in range(MB):
        for e in range(2):
            own_x[m, e] = pltpu.make_async_copy(
                x_hbm.at[0, m, :, pl.ds(feature(e, y), HALF)],
                xg.at[m, y, :, pl.ds(e * HALF, HALF)],
                loc.at[2 + 2 * m + e],
            )
            own_x[m, e].start()

    own_rows = pltpu.make_async_copy(
        x_hbm.at[0, :, :, pl.ds(pl.multiple_of(t * 4096, 4096), 4096)], rowx, loc.at[8]
    )
    own_rows.start()

    barrier = pltpu.get_barrier_semaphore()
    peers = [at(x, (y + k) % 4, (t + e) % 2) for k, e in stat_peers]
    peers += [inner, outer, ((sec + 1) % 4, dp, t), ((sec + 3) % 4, dp, t)]
    peers += [((sec + 2) % 4, dp, 1 - t)]
    for dev in peers:
        pl.semaphore_signal(barrier, inc=1, device_id=dev, device_id_type=MESH)
    own_c.wait()
    for m in range(MB):
        kept = keep[0, m].astype(F32)
        cg[m, t, y] = (cot[m].astype(F32) * kept).astype(BF16)
    pl.semaphore_wait(barrier, len(peers))

    sends = []

    def go(cp):
        cp.start()
        sends.append(cp)
        return cp

    def send_cot(m, half, i, col, origin, k):
        return go(
            remote(
                cg.at[m, col, origin], cg.at[m, col, origin],
                cs.at[m, half, i], cr.at[m, half, i], yp(k),
            )
        )

    cat = {}
    zc = {}

    def send_z(m):
        zc[m] = go(remote(cg.at[m, t, y], cg.at[m, t, y], zs.at[m], zr.at[m], zp))

    def send_own(m):
        cat[m, 0, 0] = send_cot(m, 0, 0, t, y, 1)
        cat[m, 0, 1] = send_cot(m, 0, 1, t, y, 3)

    def send_other(m):
        zc[m].wait_recv()
        cat[m, 1, 0] = send_cot(m, 1, 0, 1 - t, y, 1)
        cat[m, 1, 1] = send_cot(m, 1, 1, 1 - t, y, 3)

    def pass_own(m):
        wait_cot((m, 0, 0))
        cat[m, 0, 2] = send_cot(m, 0, 2, t, down, 1)

    def pass_other(m):
        wait_cot((m, 1, 1))
        cat[m, 1, 2] = send_cot(m, 1, 2, 1 - t, up, 3)

    up, down = (y + 1) % 4, (y + 3) % 4
    got = set()

    def wait_cot(key):
        if key not in got:
            got.add(key)
            cat[key].wait_recv()

    pieces = [(p, 128 * n, 128) for p in range(2) for n in range(4)]
    wcross, win, wout = {}, {}, {}
    for n, (p, first, size) in enumerate(pieces):
        rows = pl.ds(first, size)
        if p:
            wcross[n] = remote(
                w_hbm.at[0, rows], wg.at[odd, t, rows], ps.at[n], pr.at[n], zp
            )
        block = wg.at[here, 1 - t if p else t, rows]
        win[n] = remote(block, block, ws.at[n, 0], wr.at[n, 0], inner)
        wout[n] = remote(block, block, ws.at[n, 1], wr.at[n, 1], outer)

    def weight_step(n):
        if n in wcross:
            @pl.when(holds)
            def _():
                wcross[n].wait_recv()
                wout[n].start()
                win[n].start()

        @pl.when(lacks)
        def _():
            wout[n].wait_recv()
            win[n].start()

    xat = {}

    def send_x(m, h):
        for i, k in enumerate(ORDER):
            for e in range(2):
                start = pl.multiple_of(feature(e, (y + k) % 4) + h * 256, 256)
                xat[m, h, i, e] = go(
                    remote(
                        x_hbm.at[0, m, :, pl.ds(start, 256)],
                        xg.at[m, y, :, pl.ds(e * HALF + h * 256, 256)],
                        xs.at[m, h, i, e], xr.at[m, h, i, e], yp(k),
                    )
                )

    @pl.when(holds)
    def _():
        own_w.wait()
        for n in range(4):
            wout[n].start()
            win[n].start()

    for m in range(MB):
        send_z(m)
        send_own(m)

    @pl.when(lacks)
    def _():
        for cp in wcross.values():
            cp.start()

    lane_row = lax.broadcasted_iota(jnp.int32, (8, 128), 0)
    ones = jnp.ones((8, 128), F32)
    first_row = jnp.where(lane_row == 0, 1.0, 0.0).astype(F32)
    me = 2 * y + t

    def tell(src, slots, ssem, rsem):
        return [
            go(
                remote(
                    src, slots, ssem.at[i], rsem.at[i], at(x, (y + k) % 4, (t + e) % 2)
                )
            )
            for i, (k, e) in enumerate(stat_peers)
        ]

    own_rows.wait()
    for m in range(MB):

        def square(i, total):
            xf = rowx[m, :, pl.ds(pl.multiple_of(i * 512, 512), 512)].astype(F32)
            xf = xf * xf
            return total + (xf[:, :128] + xf[:, 128:256]) + (xf[:, 256:384] + xf[:, 384:])

        total = lax.fori_loop(0, 8, square, jnp.zeros((ROWS, 128), F32))
        squares[me, :, m * ROWS : (m + 1) * ROWS] = exact(ones, total, ((1,), (1,)))
    sums = tell(squares.at[me], squares.at[me], qs, qr)

    weight_step(0)
    send_other(0)
    pass_own(0)
    weight_step(1)
    send_other(1)
    pass_own(1)
    send_x(0, 0)
    weight_step(2)
    weight_step(3)
    pass_other(0)
    send_x(0, 1)
    weight_step(4)
    pass_other(1)
    send_x(1, 0)
    weight_step(5)
    weight_step(6)
    weight_step(7)

    for cp in sums:
        cp.wait_recv()
    for n in range(4):
        total = squares[2 * n] + squares[2 * n + 1]
        inv = lax.rsqrt(total * (1.0 / D) + EPSILON)
        wide = exact(inv, first_row, ((0,), (0,)))
        for m in range(MB):
            invb[m, n] = wide[m * ROWS : (m + 1) * ROWS]

    def cotangent(m):
        for half in range(2):
            for i in range(3):
                wait_cot((m, half, i))

    def multiply(m, h):
        if m == 0:
            for n in (0, 1, 4, 5):
                win[n + 2 * h].wait_recv()

        def tile(e, carry):
            rows = pl.ds(h * 256, 256)
            cols = pl.ds(pl.multiple_of(e * HALF + h * 256, 256), 256)
            ng = nt(cg[m, 0].reshape(HALF, HALF), wg[e, 0, rows, :])
            ng += nt(cg[m, 1].reshape(HALF, HALF), wg[e, 1, rows, :])
            start = pl.multiple_of(feature(e, y) + h * 256, 256)
            scaled[m, :, cols] = ng * gain[0:1, pl.ds(start, 256)]
            return carry

        lax.fori_loop(0, 2, tile, 0)

    def inputs(m, h):
        if h == 0:
            for e in range(2):
                own_x[m, e].wait()
        for e in range(2):
            for i in range(3):
                xat[m, h, i, e].wait_recv()
        inv = invb[m].reshape(HALF, 128)

        def tile(i, carry):
            at_col = pl.multiple_of((i // 2) * HALF + h * 256 + (i % 2) * 128, 128)
            cols = pl.ds(at_col, 128)
            start = pl.multiple_of(feature(i // 2, y) + h * 256 + (i % 2) * 128, 128)
            xf = xg[m, :, :, cols].reshape(HALF, 128).astype(F32)
            normed[m, :, cols] = (xf * inv * gain[0:1, pl.ds(start, 128)]).astype(BF16)
            return carry

        lax.fori_loop(0, 4, tile, 0)

    def dots(m, h):
        if h == 0:
            acc[...] = jnp.zeros_like(acc)

        def tile(i, carry):
            at_col = pl.multiple_of((i // 2) * HALF + h * 256 + (i % 2) * 128, 128)
            cols = pl.ds(at_col, 128)
            xf = xg[m, :, :, cols].reshape(HALF, 128).astype(F32)
            acc[...] += xf * scaled[m, :, cols]
            return carry

        lax.fori_loop(0, 4, tile, 0)

    def share(m):
        stat[m, me] = exact(ones, acc[...], ((1,), (1,)))
        return tell(stat.at[m, me], stat.at[m, me], ts.at[m], tr.at[m])

    def coefficients(m, arrivals):
        for cp in arrivals:
            cp.wait_recv()
        total = jnp.sum(stat[m], axis=0) * (1.0 / D)
        wide = exact(total, first_row, ((0,), (0,)))
        inv = invb[m].reshape(HALF, 128)
        coefb[m] = (inv * inv * inv * wide).reshape(4, ROWS, 128)

    below = ((sec + 3) % 4, dp, t)
    chained = {}
    final = {}
    spots = (2, 1, 3, 0)
    for m in range(MB):
        for i, k in enumerate(spots):
            yb = (y + k) % 4
            b = m * 4 + i
            chained[m, i] = remote(sb.at[m, yb], ci.at[b], hs.at[b], hr.at[b], below)
            for e in range(2):
                src = sb.at[m, yb, :, pl.ds(e * HALF, HALF)]
                spot = s_out.at[m, :, pl.ds(pl.multiple_of(e * 2048 + y * HALF, HALF), HALF)]
                if k:
                    final[m, i, e] = remote(src, spot, as_.at[m, i, e], ar.at[m, i, e], yp(k))
                else:
                    final[m, i, e] = pltpu.make_async_copy(src, spot, loc.at[2 + 2 * m + e])

    hops = {}
    for m in range(MB):
        yb = (y + spots[3]) % 4
        hops[m, 0] = remote(sb.at[m, yb], via.at[m, 0], vs.at[m, 0], vr.at[m, 0], (0, dp, 1 - t))
        hops[m, 1] = remote(via.at[m, 0], via.at[m, 1], vs.at[m, 1], vr.at[m, 1], (3, dp, t))
        hops[m, 2] = remote(
            via.at[m, 1], ci.at[m * 4 + 3], vs.at[m, 2], hr.at[m * 4 + 3], (1, dp, 1 - t)
        )

    def forward(m, n):
        @pl.when(sec == (0 if n == 0 else 3))
        def _():
            hops[m, n].wait_recv()
            hops[m, n + 1].start()

    def chain(m, i):
        yb = (y + spots[i]) % 4
        cp = chained[m, i]
        rows = pl.ds(pl.multiple_of(yb * ROWS, ROWS), ROWS)

        def put(above):
            def tile(n, carry):
                cols = pl.ds(pl.multiple_of(n * 128, 128), 128)
                xf = xg[m, yb, :, cols].astype(F32)
                value = invb[m, yb] * scaled[m, rows, cols] - xf * coefb[m, yb]
                if above:
                    value += ci[m * 4 + i, :, cols].astype(F32)
                sb[m, yb, :, cols] = value.astype(BF16)
                return carry

            lax.fori_loop(0, 8, tile, 0)

        @pl.when(sec < 3)
        def _():
            cp.wait_recv()
            put(True)

        @pl.when(sec == 3)
        def _():
            put(False)

        if i == 3:
            @pl.when(sec % 2 == 1)
            def _():
                cp.start()

            @pl.when(sec == 2)
            def _():
                hops[m, 0].start()

        else:
            @pl.when(sec > 0)
            def _():
                cp.start()

    def deliver(m, i):
        for e in range(2):
            final[m, i, e].start()

    def product(block, p, h):
        col = 1 - t if p == 0 else t
        cols = pl.ds(pl.multiple_of(block * HALF + h * 256, 256), 256)
        total = tn(normed[0, :, cols], cg[0, col].reshape(HALF, HALF))
        total += tn(normed[1, :, cols], cg[1, col].reshape(HALF, HALF))
        return total

    steps = [(p, h) for h in range(2) for p in range(2)]
    rin, rout, ret, kept_here = {}, {}, {}, {}
    for p, h in steps:
        i = 2 * p + h
        rin[p, h] = remote(rsi.at[i], opp.at[i], rs.at[i], rr.at[i], inner)
        rout[p, h] = remote(rso.at[i], rsr.at[i], os_.at[i], or_.at[i], outer)
    for h in range(2):
        ret[h] = remote(fb.at[h], w_out.at[part[h]], bs.at[h], br.at[h], zp)
        kept_here[h] = pltpu.make_async_copy(fb.at[2 + h], w_out.at[part[h]], loc.at[6 + h])

    def weights(h):
        for p in range(2):
            i = 2 * p + h
            rsi[i] = product(1 - here, p, h).astype(BF16)
            go(rin[p, h])
            wp[i] = product(here, p, h)

    def relay(p, h):
        i = 2 * p + h
        rin[p, h].wait_recv()

        @pl.when(lacks)
        def _():
            rso[i] = (wp[i] + opp[i].astype(F32)).astype(BF16)
            rout[p, h].start()

    def settle(p, h):
        i = 2 * p + h

        @pl.when(holds)
        def _():
            rout[p, h].wait_recv()
            fb[i] = (wp[i] + opp[i].astype(F32) + rsr[i].astype(F32)).astype(BF16)
            if p == 0:
                ret[h].start()
            else:
                kept_here[h].start()

    blocks = range(4)

    def block(m, i):
        chain(m, i)
        deliver(m, i)

    cotangent(0)
    multiply(0, 0)
    inputs(0, 0)
    dots(0, 0)
    inputs(0, 1)
    multiply(0, 1)
    dots(0, 1)
    arrivals = share(0)
    send_x(1, 1)
    cotangent(1)
    inputs(1, 0)
    weights(0)
    coefficients(0, arrivals)

    @pl.when(sec >= 2)
    def _():
        for i in (3, 0, 1, 2):
            chain(0, i)

    multiply(1, 0)
    multiply(1, 1)
    dots(1, 0)
    inputs(1, 1)
    dots(1, 1)
    arrivals = share(1)
    weights(1)
    relay(*steps[0])

    @pl.when(sec >= 2)
    def _():
        for i in blocks:
            deliver(0, i)

    @pl.when(sec < 2)
    def _():
        forward(0, 0)
        block(0, 0)
        block(0, 1)

    coefficients(1, arrivals)

    @pl.when(sec >= 2)
    def _():
        for i in (3, 0, 1, 2):
            chain(1, i)
            deliver(1, i)
        forward(0, 1)
        relay(*steps[1])
        settle(*steps[0])
        relay(*steps[2])
        settle(*steps[1])
        forward(1, 1)
        relay(*steps[3])
        settle(*steps[2])
        settle(*steps[3])

    @pl.when(sec < 2)
    def _():
        relay(*steps[1])
        block(0, 2)
        forward(1, 0)
        settle(*steps[0])
        block(0, 3)
        relay(*steps[2])
        settle(*steps[1])
        block(1, 0)
        block(1, 1)
        relay(*steps[3])
        settle(*steps[2])
        block(1, 2)
        block(1, 3)
        settle(*steps[3])

    for (m, i, e), cp in final.items():
        if i < 3:
            cp.wait_recv()
            cp.wait_send()
        else:
            cp.wait()
    for cp in sends + list(win.values()):
        cp.wait_send()

    @pl.when(holds)
    def _():
        for cp in list(wout.values()) + list(ret.values()):
            cp.wait_send()
        for h in range(2):
            kept_here[h].wait()

    @pl.when(lacks)
    def _():
        for cp in list(wcross.values()) + list(rout.values()):
            cp.wait_send()
        for h in range(2):
            ret[h].wait_recv()

    @pl.when(sec > 0)
    def _():
        for (m, i), cp in chained.items():
            if i < 3:
                cp.wait_send()

    for n, sender in enumerate((2, 0, 3)):

        @pl.when(sec == sender)
        def _():
            for m in range(MB):
                hops[m, n].wait_send()

    @pl.when(sec % 2 == 1)
    def _():
        for m in range(MB):
            chained[m, 3].wait_send()


def finish(factor, top, sums, weight, grads, scaled):
    grads[...] = top[...].astype(F32) + sums[...].astype(F32)
    scaled[...] = weight[...].astype(F32) * factor


def on_device(layer_inputs, value_cotangent, value_weight, norm_gain, skip_keep, top_grad):
    any_ = pl.BlockSpec(memory_space=pl.ANY)
    dma = pltpu.SemaphoreType.DMA
    sums, weight = pl.pallas_call(
        kernel,
        name="backward",
        out_shape=(
            jax.ShapeDtypeStruct((MB, ROWS, 4096), BF16),
            jax.ShapeDtypeStruct((HALF, HALF), BF16),
        ),
        in_specs=[
            any_, any_, any_,
            pl.BlockSpec(memory_space=pltpu.VMEM),
            pl.BlockSpec(memory_space=pltpu.SMEM),
        ],
        out_specs=(any_, any_),
        scratch_shapes=[
            pltpu.VMEM((MB, ROWS, HALF), BF16),
            pltpu.VMEM((MB, ROWS, 4096), BF16),
            pltpu.VMEM((MB, 2, 4, ROWS, HALF), BF16),
            pltpu.VMEM((2, 2, HALF, HALF), BF16),
            pltpu.VMEM((MB, 4, ROWS, SUB), BF16),
            pltpu.VMEM((MB, HALF, SUB), F32),
            pltpu.VMEM((MB, HALF, SUB), BF16),
            pltpu.VMEM((HALF, 128), F32),
            pltpu.VMEM((MB, 4, ROWS, 128), F32),
            pltpu.VMEM((MB, 4, ROWS, 128), F32),
            pltpu.VMEM((8, 8, 2 * ROWS), F32),
            pltpu.VMEM((MB, 8, 8, HALF), F32),
            pltpu.VMEM((4, 256, HALF), F32),
            pltpu.VMEM((4, 256, HALF), BF16),
            pltpu.VMEM((4, 256, HALF), BF16),
            pltpu.VMEM((4, 256, HALF), BF16),
            pltpu.VMEM((4, 256, HALF), BF16),
            pltpu.VMEM((4, 256, HALF), BF16),
            pltpu.VMEM((MB, 4, ROWS, SUB), BF16),
            pltpu.VMEM((8, ROWS, SUB), BF16),
            pltpu.VMEM((MB, 2, ROWS, SUB), BF16),
            dma((9,)),
            dma((7,)), dma((7,)),
            dma((MB,)), dma((MB,)),
            dma((MB, 2, 3)), dma((MB, 2, 3)),
            dma((MB, 2, 3, 2)), dma((MB, 2, 3, 2)),
            dma((8,)), dma((8,)),
            dma((8, 2)), dma((8, 2)),
            dma((MB, 7)), dma((MB, 7)),
            dma((8,)), dma((8,)),
            dma((MB, 3)), dma((MB, 2)),
            dma((MB, 3, 2)), dma((MB, 3, 2)),
            dma((4,)), dma((4,)),
            dma((4,)), dma((4,)),
            dma((2,)), dma((2,)),
        ],
        compiler_params=pltpu.CompilerParams(
            collective_id=0, has_side_effects=True, vmem_limit_bytes=56 * 1024 * 1024
        ),
    )(layer_inputs, value_cotangent, value_weight, norm_gain, skip_keep.reshape(1, MB))
    total_rows = MB * ROWS * lax.axis_size("dp")
    factor = float(total_rows) ** (-0.5)
    rows, cols = MB * ROWS // 2, HALF // 2
    grads, scaled = pl.pallas_call(
        functools.partial(finish, factor),
        name="finish",
        out_shape=(
            jax.ShapeDtypeStruct((MB * ROWS, 4096), F32),
            jax.ShapeDtypeStruct((HALF, HALF), F32),
        ),
        grid=(2,),
        in_specs=[
            pl.BlockSpec((rows, 4096), lambda i: (i, 0)),
            pl.BlockSpec((rows, 4096), lambda i: (i, 0)),
            pl.BlockSpec((cols, HALF), lambda i: (i, 0)),
        ],
        out_specs=(
            pl.BlockSpec((rows, 4096), lambda i: (i, 0)),
            pl.BlockSpec((cols, HALF), lambda i: (i, 0)),
        ),
    )(top_grad.reshape(MB * ROWS, 4096), sums.reshape(MB * ROWS, 4096), weight)
    return grads.reshape(1, MB, ROWS, 4096), scaled[None]


def solution(mesh):
    placed = (
        P("section", None, "dp", None),
        P("section", None, "dp", "tensor"),
        P("section", "dp", "tensor"),
        P("section", None),
        P("section", None, "dp"),
        P(None, "dp", "tensor"),
    )
    return jax.shard_map(
        on_device,
        mesh=mesh,
        in_specs=placed,
        out_specs=(P("section", None, "dp", "tensor"), P("section", "dp", "tensor")),
        check_vma=False,
    )
```
